768 devices in a mesh: row: 32 (over x_hi, y, core), col: 24 (over z, x_lo).
Axes of the slice: x: 4 (x_hi: 2, x_lo: 2; x = x_hi * 2 + x_lo), y: 8, z: 12, core: 2. Of those that a mesh axis runs over, the one named last changes fastest.
Arguments:
- design_rows: bfloat16 [768, 12288], P('col', 'row'), may hold values from -1.1953125 to 1.1953125
- design_cols: bfloat16 [768, 24576], P('row', 'col'), may hold values from -1.1953125 to 1.1953125
- whitening: bfloat16 [768, 768], replicated, may hold values from -16 to 16, as said below
- epoch_mask: int32 [128], replicated, may hold values 0 or 1
- normal_old: float32 [12288, 24576], P('row', 'col'), may hold values from -6 to 6
- probes: float32 [24576, 64], P('col'), may hold values from -0.0390625 to 0.0390625
Outputs:
- normal_new: float32 [12288, 24576], P('row', 'col')
- products: float32 [12288, 64], P(('row', 'col'))
The draws below stay inside these ranges and needn't reach their ends.
Inputs may be any that keep to these rules, and one draw needn't show every extreme that they name: `whitening`: lower triangular with a positive diagonal.
All inputs are finite; a program needn't handle non-finite values.
Results may differ from the reference program's by a relative error of at most 0.0028.
Values may be sent and summed in bfloat16 or wider, within the bound.
A program may use at most 32 MiB of HBM per device.

```python
import jax
import jax.numpy as jnp
from jax import lax

EPOCHS = 128
COMP = 6
M = 768
PROBES = 64
NR = 12288
NC = 24576


def draw_whitening(key, part):
    count = EPOCHS * COMP
    first = jax.random.fold_in(key, 11)
    second = jax.random.fold_in(key, 12)
    lower = jnp.clip(jax.random.normal(first, (count, count), jnp.float32), -4.0, 4.0)
    lower = jnp.tril(lower, -1) * (0.6 / jnp.sqrt(jnp.float32(count)))
    diag_part = 1.0 + jax.random.uniform(second, (count,), jnp.float32)
    matrix = lower + jnp.diag(diag_part)
    return matrix.astype(jnp.bfloat16)


def plant(values, rng, least, top_value):
    shape = values.shape
    place = [jax.random.randint(jax.random.fold_in(rng, axis), (), 0, shape[axis]) for axis in range(len(shape))]
    values = values.at[tuple(place)].set(least)
    longest = shape.index(max(shape))
    place[longest] = (place[longest] + 1) % shape[longest]
    return values.at[tuple(place)].set(top_value)


def shard_levels(key, dims, shards, least, top_value):
    factor_of = 1.0
    for axis_at, parts in shards:
        steps = jax.random.uniform(jax.random.fold_in(jax.random.fold_in(key, 6), axis_at), (parts,), jnp.float32, least / len(shards), top_value / len(shards))
        factor_of = factor_of * jnp.repeat(jnp.exp(steps), dims[axis_at] // parts).reshape((-1,) + (1,) * (len(dims) - 1 - axis_at))
    return factor_of


def normal_values(key, shape, deviation, reach, cuts=(), held_as=jnp.bfloat16):
    array = deviation * jax.random.normal(key, shape, jnp.float32)
    if cuts:
        array = array * shard_levels(key, shape, cuts, -0.22, 0.18)
    return jnp.clip(array, -reach, reach).astype(held_as)


def setup_inputs(seed: int = 0) -> dict:
    key_of = jax.random.split(jax.random.key(seed), 7)
    return {
        "design_rows": normal_values(key_of[0], (M, NR), 0.2, 1.1953125, ((0, 24), (1, 32))),
        "design_cols": normal_values(key_of[1], (M, NC), 0.2, 1.1953125, ((0, 32), (1, 24))),
        "whitening": draw_whitening(jax.random.fold_in(key_of[6], 71), 0),
        "epoch_mask": plant((jax.random.randint(key_of[3], (EPOCHS,), 0, 4) < 3).astype(jnp.int32), jax.random.fold_in(key_of[3], 1), 0, 1),
        "normal_old": normal_values(key_of[4], (NR, NC), 1.0, 6.0, ((0, 32), (1, 24)), jnp.float32),
        "probes": normal_values(key_of[5], (NC, PROBES), NC ** -0.5, 0.0390625, ((0, 24),), jnp.float32),
    }


def reference(design_rows, design_cols, whitening, epoch_mask, normal_old, probes):
    white_rows = jnp.dot(whitening, design_rows, preferred_element_type=jnp.float32).astype(jnp.bfloat16)
    white_cols = jnp.dot(whitening, design_cols, preferred_element_type=jnp.float32)
    obs_mask = jnp.repeat(epoch_mask, COMP).astype(jnp.bfloat16)
    weighted = white_rows * obs_mask[:, None]
    gram = lax.dot_general(weighted.astype(jnp.float32), white_cols, (((0,), (0,)), ((), ())), precision=lax.Precision.HIGHEST, preferred_element_type=jnp.float32)
    normal_new = normal_old + gram
    products = jnp.dot(normal_new, probes, precision=lax.Precision.HIGHEST, preferred_element_type=jnp.float32)
    return normal_new, products
```

```python
import jax
import jax.numpy as jnp
from jax import lax
from jax.experimental import pallas as pl
from jax.experimental.pallas import tpu as pltpu
from jax.sharding import PartitionSpec as P

MESH = pl.DeviceIdType.MESH
COMP = 6
NZ, NY = 12, 8
BF, F32 = jnp.bfloat16, jnp.float32


def split2(x):
    hi = x.astype(BF)
    return hi, (x - hi.astype(F32)).astype(BF)


def dot(a, b, dims=((1,), (0,))):
    return lax.dot_general(a, b, (dims, ((), ())), preferred_element_type=F32)


class Names(dict):
    def __missing__(self, key):
        self[key] = len(self)
        return self[key]


def kernel(
    rows_h, cols_h, w_h, mask_v, old_h, prob_h, new_o, prod_o,
    R, RT, C, W, Wm, Y, OLD, PR, PB, PX, Q, G, ss, rs, ls,
):
    row, col = lax.axis_index("row"), lax.axis_index("col")
    core, y, xh = row % 2, (row // 2) % NY, row // (2 * NY)
    z, xl = col // 2, col % 2

    def at_z(k):
        return (z + k + NZ) % NZ

    def at_y(k):
        return (y + k + NY) % NY

    def to_z(k):
        return (row, at_z(k) * 2 + xl)

    def to_y(k):
        return ((xh * NY + at_y(k)) * 2 + core, col)

    to_xl = (row, z * 2 + 1 - xl)
    to_xh = (((1 - xh) * NY + y) * 2 + core, col)
    to_core = ((xh * NY + y) * 2 + 1 - core, col)

    local = [
        pltpu.make_async_copy(src, dst, ls.at[i])
        for i, (src, dst) in enumerate(
            (
                (rows_h, R.at[z, xl]),
                (cols_h, C.at[xh, y, core]),
                (w_h, W),
                (prob_h, PR),
                (old_h, OLD),
            )
        )
    ]
    for copy in local:
        copy.start()

    barrier = pltpu.get_barrier_semaphore()
    others = [to_z(k) for k in range(-5, 7) if k] + [to_y(k) for k in (-2, -1, 1, 2)] + [to_xl, to_xh, to_core]
    for other in others:
        pl.semaphore_signal(barrier, inc=1, device_id=other, device_id_type=MESH)
    pl.semaphore_wait(barrier, len(others))

    sems, sent = Names(), []

    def send(src, dst, name, device):
        copy = pltpu.make_async_remote_copy(
            src_ref=src,
            dst_ref=dst,
            send_sem=ss.at[len(sent)],
            recv_sem=rs.at[sems[name]],
            device_id=device,
            device_id_type=MESH,
        )
        copy.start()
        sent.append(copy)

    def arrive(dst, name):
        pltpu.make_async_remote_copy(
            src_ref=dst, dst_ref=dst, send_sem=ss.at[0], recv_sem=rs.at[sems[name]],
            device_id=to_core, device_id_type=MESH,
        ).wait_recv()

    def rbuf(k, side):
        return R.at[at_z(k), xl if side == 0 else 1 - xl]

    def relay_rows(k, side):
        s = 1 if k > 0 else -1
        buf = rbuf(k, side)
        send(buf, buf, ("r", 4 * s, side), to_z(-s))
        send(buf, buf, ("r", 5 * s, side), to_z(-2 * s))
        half = R.at[at_z(k), xl if side == 0 else 1 - xl, pl.ds(0 if s > 0 else 16, 16)]
        send(half, half, ("r", 6 * s, side), to_z(-3 * s))

    def rows_in(k, side):
        if k == 6:
            for s in (1, -1):
                half = R.at[at_z(k), xl if side == 0 else 1 - xl, pl.ds(0 if s > 0 else 16, 16)]
                arrive(half, ("r", 6 * s, side))
        else:
            arrive(rbuf(k, side), ("r", k, side))

    def cbuf(k, side, sibling=False):
        return C.at[xh if side == 0 else 1 - xh, at_y(k), 1 - core if sibling else core]

    def chalf(k, side, s):
        return C.at[xh if side == 0 else 1 - xh, at_y(k), core, :, pl.ds(0 if s > 0 else 512, 512)]

    def relay_cols(k, side):
        s = 1 if k > 0 else -1
        buf = cbuf(k, side)
        send(buf, buf, ("c", 3 * s, side), to_y(-s))
        half = chalf(k, side, s)
        send(half, half, ("c", 4 * s, side), to_y(-2 * s))

    def cols_in(k, side):
        if k == 4:
            for s in (1, -1):
                arrive(chalf(k, side, s), ("c", 4 * s, side))
        else:
            arrive(cbuf(k, side), ("c", k, side))

    def to_sibling(k, side):
        buf = cbuf(k, side)
        send(buf, buf, ("s", k, side), to_core)

    def from_sibling(k, side):
        arrive(cbuf(k, side, True), ("s", k, side))

    def cross_rows(k):
        buf = rbuf(k, 0)
        send(buf, buf, ("r", k, 1), to_xl)

    def cross_cols(k):
        buf = cbuf(k, 0)
        send(buf, buf, ("c", k, 1), to_xh)

    own_r, own_c = R.at[z, xl], C.at[xh, y, core]
    for k in (3, -3, 2, -2, 1, -1):
        if abs(k) == 2:
            send(cols_h, own_c, ("c", -k, 0), to_y(k))
        if abs(k) == 1:
            send(cols_h, own_c, ("c", -k, 0), to_y(k))
        send(rows_h, own_r, ("r", -k, 0), to_z(k))
    send(cols_h, own_c, ("c", 0, 1), to_xh)
    send(rows_h, own_r, ("r", 0, 1), to_xl)
    send(cols_h, own_c, ("s", 0, 0), to_core)

    for copy in local[2:4]:
        copy.wait()
    obs = lax.broadcasted_iota(jnp.int32, (768, 128), 0)
    first = COMP * lax.broadcasted_iota(jnp.int32, (768, 128), 1)
    keep = (obs >= first) & (obs < first + COMP)
    mask = jnp.sum(jnp.where(keep, mask_v[...].astype(F32), 0.0), axis=1, keepdims=True)
    Wm[...] = W[...] * mask.astype(BF)

    for k in (1, -1):
        rows_in(k, 0)
        cross_rows(k)
    for k in (2, -2):
        cols_in(k, 0)
        relay_cols(k, 0)
        cross_cols(k)
    for k in (3, -3):
        rows_in(k, 0)
        relay_rows(k, 0)
        cross_rows(k)
    for k in (1, -1):
        cols_in(k, 0)
        cross_cols(k)
    for k in (2, -2):
        rows_in(k, 0)
        cross_rows(k)
    cols_in(0, 1)
    for k in (1, -1, 2, -2):
        to_sibling(k, 0)
    to_sibling(0, 1)
    for k in (2, -2):
        cols_in(k, 1)
        relay_cols(k, 1)
    for k in (3, -3):
        rows_in(k, 1)
        relay_rows(k, 1)
    for k in (1, -1):
        cols_in(k, 1)
    for k in (1, -1, 2, -2):
        to_sibling(k, 1)
    for k in (3, -3, 4):
        cols_in(k, 0)
        to_sibling(k, 0)
    for k in (0, 1, -1, 2, -2):
        rows_in(k, 1)
    for side in (0, 1):
        for k in (4, -4, 5, -5, 6):
            rows_in(k, side)
    local[0].wait()
    local[1].wait()
    local[4].wait()

    for b in range(6):
        block = R[2 * b : 2 * b + 2].reshape(128, 384)
        RT[:, 128 * b : 128 * b + 128] = block.T
    white = dot(RT[...], W[...], ((1,), (1,))).astype(BF)
    full = dot(white, Wm[...])
    hi, lo = split2(full)
    for h in range(2):
        Y[h, :384] = hi[:, 384 * h : 384 * h + 384]
        Y[h, 384:] = lo[:, 384 * h : 384 * h + 384]

    def gram(h):
        def tile(n, _):
            at = pl.ds(pl.multiple_of(n * 256, 256), 256)
            cols = C[h, :, :, :, at].reshape(384, 256)
            both = dot(Y[h], cols)
            OLD[:, at] = OLD[:, at] + (both[:384] + both[384:])
            return 0

        lax.fori_loop(0, 4, tile, 0)

    for k in (0, 1, -1, 2, -2, 3, -3, 4):
        from_sibling(k, 0)
    gram(xh)
    for k in (3, -3, 4):
        cols_in(k, 1)
        to_sibling(k, 1)
    for k in (0, 1, -1, 2, -2, 3, -3, 4):
        from_sibling(k, 1)
    gram(1 - xh)

    new = OLD[...]
    new_o[...] = new
    hi, lo = split2(new)
    phi, plo = split2(PR[...])
    both = jnp.concatenate([phi, plo], axis=0)
    part = dot(hi, both, ((1,), (1,)))
    low = dot(lo, phi, ((1,), (1,)))
    part = part[:, :64] + part[:, 64:] + low
    part = part.reshape(48, 8, 64).reshape(24, 2, 8, 64)
    PB[...] = jnp.concatenate([part[:, 0], part[:, 1]], axis=-1).reshape(NZ, 2, 8, 128)

    send(PB.at[:, 1 - xl], PX, ("px",), to_xl)
    arrive(PX, ("px",))
    Q[...] = PB[:, xl] + PX[...]
    for k in (6, 5, -5, 4, -4, 3, -3, 2, -2, 1, -1):
        send(Q.at[at_z(k)], G.at[k + 5], ("q", k), to_z(k))
    total = Q[z]
    for k in (1, -1, 2, -2, 3, -3, 4, -4, 5, -5, 6):
        arrive(G.at[k + 5], ("q", k))
        total = total + G[k + 5]
    prod_o[:8] = total[:, :64]
    prod_o[8:] = total[:, 64:]
    for copy in sent:
        copy.wait_send()


def body(design_rows, design_cols, whitening, epoch_mask, normal_old, probes):
    vmem = pl.BlockSpec(memory_space=pltpu.VMEM)
    hbm = pl.BlockSpec(memory_space=pl.ANY)
    return pl.pallas_call(
        kernel,
        out_shape=(
            jax.ShapeDtypeStruct((384, 1024), F32),
            jax.ShapeDtypeStruct((16, 64), F32),
        ),
        in_specs=[hbm, hbm, hbm, vmem, hbm, hbm],
        out_specs=(vmem, vmem),
        scratch_shapes=[
            pltpu.VMEM((NZ, 2, 32, 384), BF),
            pltpu.VMEM((384, 768), BF),
            pltpu.VMEM((2, NY, 2, 24, 1024), BF),
            pltpu.VMEM((768, 768), BF),
            pltpu.VMEM((768, 768), BF),
            pltpu.VMEM((2, 768, 384), BF),
            pltpu.VMEM((384, 1024), F32),
            pltpu.VMEM((64, 1024), F32),
            pltpu.VMEM((NZ, 2, 8, 128), F32),
            pltpu.VMEM((NZ, 8, 128), F32),
            pltpu.VMEM((NZ, 8, 128), F32),
            pltpu.VMEM((NZ, 8, 128), F32),
            pltpu.SemaphoreType.DMA((96,)),
            pltpu.SemaphoreType.DMA((96,)),
            pltpu.SemaphoreType.DMA((5,)),
        ],
        compiler_params=pltpu.CompilerParams(
            collective_id=0, has_side_effects=True, vmem_limit_bytes=48 * 2**20
        ),
        name="normal_update",
    )(
        design_rows,
        design_cols,
        whitening,
        epoch_mask.reshape(1, 128),
        normal_old,
        probes.T,
    )


def solution(mesh):
    placed = (P("col", "row"), P("row", "col"), P(), P(), P("row", "col"), P("col", None))
    return jax.shard_map(
        body,
        mesh=mesh,
        in_specs=placed,
        out_specs=(P("row", "col"), P(("row", "col"), None)),
        check_vma=False,
    )
```

```python
import jax
import jax.numpy as jnp
from jax import lax
from jax.experimental import pallas as pl
from jax.experimental.pallas import tpu as pltpu
from jax.sharding import PartitionSpec as P

MESH = pl.DeviceIdType.MESH
COMP = 6
NZ, NY = 12, 8
BF, F32 = jnp.bfloat16, jnp.float32


def split2(x):
    hi = x.astype(BF)
    return hi, (x - hi.astype(F32)).astype(BF)


def dot(a, b, dims=((1,), (0,))):
    return lax.dot_general(a, b, (dims, ((), ())), preferred_element_type=F32)


def pack(x):
    return jnp.concatenate(split2(x), axis=-1)


def unpack(x):
    x = x.astype(F32)
    return x[..., :64] + x[..., 64:]


class Names(dict):
    def __missing__(self, key):
        self[key] = len(self)
        return self[key]


def kernel(
    rows_h, cols_h, w_h, mask_v, old_h, prob_h, new_o, prod_o,
    R, RT, C, W, Wm, Y, OLD, PR, PB, PX, Q, QB, QR, GX, GS, GZ, GF, ss, rs, ls,
):
    row, col = lax.axis_index("row"), lax.axis_index("col")
    core, y, xh = row % 2, (row // 2) % NY, row // (2 * NY)
    z, xl = col // 2, col % 2

    def at_z(k):
        return (z + k + NZ) % NZ

    def at_y(k):
        return (y + k + NY) % NY

    def to_z(k):
        return (row, at_z(k) * 2 + xl)

    def to_y(k):
        return ((xh * NY + at_y(k)) * 2 + core, col)

    other_row = ((1 - xh) * NY + y) * 2 + core
    to_xl = (row, z * 2 + 1 - xl)
    to_xh = (other_row, col)
    to_diagonal = (other_row, z * 2 + 1 - xl)
    to_core = ((xh * NY + y) * 2 + 1 - core, col)

    barrier = pltpu.get_barrier_semaphore()
    others = [to_z(k) for k in range(-5, 7) if k] + [to_y(k) for k in range(-3, 5) if k]
    others += [to_xl, to_xh, to_diagonal, to_core]
    for other in others:
        pl.semaphore_signal(barrier, inc=1, device_id=other, device_id_type=MESH)

    local = [
        pltpu.make_async_copy(src, dst, ls.at[i])
        for i, (src, dst) in enumerate(
            (
                (cols_h, C.at[xh, y, core]),
                (prob_h, PR),
                (rows_h, R.at[z, xl]),
                (w_h, W),
                (old_h, OLD),
            )
        )
    ]
    for copy in local:
        copy.start()
    pl.semaphore_wait(barrier, len(others))

    sems, sent = Names(), []

    def send(src, dst, name, device):
        copy = pltpu.make_async_remote_copy(
            src_ref=src,
            dst_ref=dst,
            send_sem=ss.at[len(sent)],
            recv_sem=rs.at[sems[name]],
            device_id=device,
            device_id_type=MESH,
        )
        copy.start()
        sent.append(copy)

    def arrive(dst, name):
        pltpu.make_async_remote_copy(
            src_ref=dst, dst_ref=dst, send_sem=ss.at[0], recv_sem=rs.at[sems[name]],
            device_id=to_core, device_id_type=MESH,
        ).wait_recv()

    def rbuf(k, side):
        return R.at[at_z(k), xl if side == 0 else 1 - xl]

    def rhalf(k, side, s):
        return R.at[at_z(k), xl if side == 0 else 1 - xl, pl.ds(0 if s > 0 else 16, 16)]

    def relay_rows(k, side):
        s = 1 if k > 0 else -1
        buf, half = rbuf(k, side), rhalf(k, side, s)
        send(half, half, ("r", 6 * s, side), to_z(-3 * s))
        send(buf, buf, ("r", 5 * s, side), to_z(-2 * s))
        send(buf, buf, ("r", 4 * s, side), to_z(-s))

    def rows_in(k, side):
        if k == 6:
            for s in (1, -1):
                arrive(rhalf(k, side, s), ("r", 6 * s, side))
        else:
            arrive(rbuf(k, side), ("r", k, side))

    def cbuf(k, side, sibling=False):
        return C.at[xh if side == 0 else 1 - xh, at_y(k), 1 - core if sibling else core]

    def chalf(k, side, s):
        return C.at[xh if side == 0 else 1 - xh, at_y(k), core, :, pl.ds(0 if s > 0 else 512, 512)]

    def relay_cols(k, side):
        s = 1 if k > 0 else -1
        buf, half = cbuf(k, side), chalf(k, side, s)
        send(half, half, ("c", 4 * s, side), to_y(-2 * s))
        send(buf, buf, ("c", 3 * s, side), to_y(-s))

    def cols_in(k, side):
        if k == 4:
            for s in (1, -1):
                arrive(chalf(k, side, s), ("c", 4 * s, side))
        else:
            arrive(cbuf(k, side), ("c", k, side))

    def to_sibling(k, side):
        buf = cbuf(k, side)
        send(buf, buf, ("s", k, side), to_core)

    def from_sibling(k, side):
        arrive(cbuf(k, side, True), ("s", k, side))

    def cross_rows(k):
        buf = rbuf(k, 0)
        send(buf, buf, ("r", k, 1), to_xl)

    def cross_cols(k):
        buf = cbuf(k, 0)
        send(buf, buf, ("c", k, 1), to_xh)

    own_r, own_c = R.at[z, xl], C.at[xh, y, core]
    send(rows_h, own_r, ("r", -3, 0), to_z(3))
    send(rows_h, own_r, ("r", 3, 0), to_z(-3))
    send(cols_h, own_c, ("c", -2, 0), to_y(2))
    send(cols_h, own_c, ("c", 2, 0), to_y(-2))
    send(cols_h, own_c, ("c", 0, 1), to_xh)
    send(rows_h, own_r, ("r", 0, 1), to_xl)
    for k in (1, -1):
        send(cols_h, own_c, ("c", -k, 0), to_y(k))
        send(rows_h, own_r, ("r", -k, 0), to_z(k))
    for k in (2, -2):
        send(rows_h, own_r, ("r", -k, 0), to_z(k))
    send(cols_h, own_c, ("s", 0, 0), to_core)

    local[0].wait()
    local[1].wait()
    phi, plo = split2(PR[...])
    both = jnp.concatenate([phi, plo], axis=0)
    share = unpack(dot(C[xh, y, core], both, ((1,), (1,))))
    GS[0, 0] = pack(share)
    for i, device in enumerate((to_xl, to_xh, to_diagonal)):
        send(GS.at[0, 0], GX.at[i], ("gx", i), device)

    local[3].wait()
    obs = lax.broadcasted_iota(jnp.int32, (768, 128), 0)
    first = COMP * lax.broadcasted_iota(jnp.int32, (768, 128), 1)
    keep = (obs >= first) & (obs < first + COMP)
    mask = jnp.sum(jnp.where(keep, mask_v[...].astype(F32), 0.0), axis=1, keepdims=True)
    Wm[...] = W[...] * mask.astype(BF)

    for k in (1, -1):
        rows_in(k, 0)
        cross_rows(k)
    for k in (2, -2):
        cols_in(k, 0)
        relay_cols(k, 0)
        cross_cols(k)
    for k in (3, -3):
        rows_in(k, 0)
        relay_rows(k, 0)
        cross_rows(k)

    for i in range(3):
        arrive(GX.at[i], ("gx", i))
    mine = share + unpack(GX[0])
    theirs = unpack(GX[1]) + unpack(GX[2])
    GS[1, 0] = pack(mine)
    GS[1, 1] = pack(theirs)
    for i, k in enumerate((1, -1)):
        send(GS.at[1], GZ.at[i], ("gz", i), to_z(k))

    for k in (1, -1):
        cols_in(k, 0)
        cross_cols(k)
    for k in (2, -2):
        rows_in(k, 0)
        cross_rows(k)
    cols_in(0, 1)
    for k in (2, -2, 1, -1):
        to_sibling(k, 0)
    to_sibling(0, 1)

    local[4].wait()
    hi, lo = split2(OLD[...])
    PB[...] = pack(unpack(dot(hi, both, ((1,), (1,)))) + dot(lo, phi, ((1,), (1,)))).reshape(NZ, 2, 16, 128)
    send(PB.at[:, 1 - xl], PX, ("px",), to_xl)

    for i in range(2):
        arrive(GZ.at[i], ("gz", i))
        mine = mine + unpack(GZ[i, 0])
        theirs = theirs + unpack(GZ[i, 1])
    GS[2, 0] = pack(mine)
    GS[2, 1] = pack(theirs)
    for i, k in enumerate((6, 3, -3)):
        send(GS.at[2], GZ.at[2 + i], ("gz", 2 + i), to_z(k))

    for k in (3, -3):
        rows_in(k, 1)
        relay_rows(k, 1)
    for k in (2, -2):
        cols_in(k, 1)
        relay_cols(k, 1)

    arrive(PX, ("px",))
    Q[...] = unpack(PB[:, xl]) + unpack(PX[...])
    QB[...] = pack(Q[...])
    for k in (6, 5, -5, 4, -4, 3, -3, 2, -2, 1, -1):
        send(QB.at[at_z(k)], QR.at[k + 5], ("q", k), to_z(k))

    for k in (2, -2):
        to_sibling(k, 1)
    for k in (3, -3, 4):
        cols_in(k, 0)
        to_sibling(k, 0)
    for k in (1, -1):
        cols_in(k, 1)
        to_sibling(k, 1)

    def turn(j):
        pair = (z // 2 + j + 6) % 6
        block = R[pl.ds(2 * pair, 2)].reshape(128, 384)
        RT[:, pl.ds(pl.multiple_of(128 * pair, 128), 128)] = block.T

    local[2].wait()
    for k in (0, 1, -1, 2, -2):
        rows_in(k, 1)
    for j in (0, 1, -1):
        turn(j)

    for i in range(2, 5):
        arrive(GZ.at[i], ("gz", i))
        mine = mine + unpack(GZ[i, 0])
        theirs = theirs + unpack(GZ[i, 1])
    GF[xh, y, core] = pack(mine)
    GF[1 - xh, y, core] = pack(theirs)
    for k in (4, 3, -3, 2, -2, 1, -1):
        send(GF.at[:, y, core], GF.at[:, y, core], ("gf", k), to_y(k))

    for side in (0, 1):
        for k in (4, -4, 5, -5, 6):
            rows_in(k, side)
    for j in (2, -2, 3):
        turn(j)

    parts = []
    for b in range(3):
        end = 256 * b + 256
        parts.append(dot(RT[:, :end], W[256 * b : end, :end], ((1,), (1,))).astype(BF))
    white = jnp.concatenate(parts, axis=1)
    parts = [dot(white[:, 256 * b :], Wm[256 * b :, 256 * b : 256 * b + 256]) for b in range(3)]
    hi, lo = split2(jnp.concatenate(parts, axis=1))
    for h in range(2):
        Y[h, :384] = hi[:, 384 * h : 384 * h + 384]
        Y[h, 384:] = lo[:, 384 * h : 384 * h + 384]

    def gram(h, old, new):
        def tile(n, _):
            at = pl.ds(pl.multiple_of(n * 256, 256), 256)
            both = dot(Y[h], C[h, :, :, :, at].reshape(384, 256))
            new[:, at] = old[:, at] + (both[:384] + both[384:])
            return 0

        lax.fori_loop(0, 4, tile, 0)

    for k in (0, 1, -1, 2, -2, 3, -3, 4):
        from_sibling(k, 0)
    for k in (3, -3, 4):
        cols_in(k, 1)
        to_sibling(k, 1)
    gram(xh, OLD, OLD)
    for k in (4, 3, -3, 2, -2, 1, -1):
        arrive(GF.at[:, at_y(-k), core], ("gf", k))
    send(GF.at[:, :, core], GF.at[:, :, core], ("gs",), to_core)
    for k in (0, 1, -1, 2, -2, 3, -3, 4):
        from_sibling(k, 1)
    gram(1 - xh, OLD, new_o)

    total = jnp.zeros((16, 128), F32)
    for k in (1, -1, 2, -2, 3, -3, 4, -4, 5, -5, 6):
        arrive(QR.at[k + 5], ("q", k))
        total = total + QR[k + 5].astype(F32)
    total = Q[z] + unpack(total)
    arrive(GF.at[:, :, 1 - core], ("gs",))
    for h in range(2):
        at = pl.multiple_of(col * 16, 16)
        for first in (0, 384):
            total = total + unpack(dot(Y[h, pl.ds(first + at, 16)], GF[h].reshape(384, 128)))
    prod_o[...] = total
    for copy in sent:
        copy.wait_send()


def write_out(new_v, prod_v, new_h, prod_h, sems):
    copies = [pltpu.make_async_copy(prod_v, prod_h, sems.at[4])]
    for i in range(4):
        rows = pl.ds(96 * i, 96)
        copies.append(pltpu.make_async_copy(new_v.at[rows], new_h.at[rows], sems.at[i]))
    for copy in copies:
        copy.start()
    for copy in copies:
        copy.wait()


def body(design_rows, design_cols, whitening, epoch_mask, normal_old, probes):
    vmem = pl.BlockSpec(memory_space=pltpu.VMEM)
    hbm = pl.BlockSpec(memory_space=pltpu.HBM)
    new, products = pl.pallas_call(
        kernel,
        out_shape=(pltpu.VMEM((384, 1024), F32), pltpu.VMEM((16, 64), F32)),
        in_specs=[hbm, hbm, hbm, vmem, hbm, hbm],
        out_specs=(vmem, vmem),
        scratch_shapes=[
            pltpu.VMEM((NZ, 2, 32, 384), BF),
            pltpu.VMEM((384, 768), BF),
            pltpu.VMEM((2, NY, 2, 24, 1024), BF),
            pltpu.VMEM((768, 768), BF),
            pltpu.VMEM((768, 768), BF),
            pltpu.VMEM((2, 768, 384), BF),
            pltpu.VMEM((384, 1024), F32),
            pltpu.VMEM((64, 1024), F32),
            pltpu.VMEM((NZ, 2, 16, 128), BF),
            pltpu.VMEM((NZ, 16, 128), BF),
            pltpu.VMEM((NZ, 16, 64), F32),
            pltpu.VMEM((NZ, 16, 128), BF),
            pltpu.VMEM((NZ, 16, 128), BF),
            pltpu.VMEM((3, 24, 128), BF),
            pltpu.VMEM((3, 2, 24, 128), BF),
            pltpu.VMEM((5, 2, 24, 128), BF),
            pltpu.VMEM((2, NY, 2, 24, 128), BF),
            pltpu.SemaphoreType.DMA((112,)),
            pltpu.SemaphoreType.DMA((112,)),
            pltpu.SemaphoreType.DMA((5,)),
        ],
        compiler_params=pltpu.CompilerParams(
            collective_id=0, has_side_effects=True, vmem_limit_bytes=56 * 2**20
        ),
        name="normal_update",
    )(
        design_rows,
        design_cols,
        whitening,
        epoch_mask.reshape(1, 128),
        normal_old,
        probes.T,
    )
    return pl.pallas_call(
        write_out,
        out_shape=(
            jax.ShapeDtypeStruct((384, 1024), F32),
            jax.ShapeDtypeStruct((16, 64), F32),
        ),
        in_specs=[vmem, vmem],
        out_specs=(hbm, hbm),
        scratch_shapes=[pltpu.SemaphoreType.DMA((5,))],
        compiler_params=pltpu.CompilerParams(vmem_limit_bytes=4 * 2**20),
        name="write_out",
    )(new, products)


def solution(mesh):
    placed = (P("col", "row"), P("row", "col"), P(), P(), P("row", "col"), P("col", None))
    return jax.shard_map(
        body,
        mesh=mesh,
        in_specs=placed,
        out_specs=(P("row", "col"), P(("row", "col"), None)),
        check_vma=False,
    )
```

```python
import jax
import jax.numpy as jnp
from jax import lax
from jax.experimental import pallas as pl
from jax.experimental.pallas import tpu as pltpu
from jax.sharding import PartitionSpec as P

MESH = pl.DeviceIdType.MESH
COMP = 6
NZ, NY = 12, 8
BF, F32 = jnp.bfloat16, jnp.float32


def split2(x):
    hi = x.astype(BF)
    return hi, (x - hi.astype(F32)).astype(BF)


def dot(a, b, dims=((1,), (0,))):
    return lax.dot_general(a, b, (dims, ((), ())), preferred_element_type=F32)


def pack(x):
    return jnp.concatenate(split2(x), axis=-1)


def unpack(x):
    x = x.astype(F32)
    return x[..., :64] + x[..., 64:]


class Names(dict):
    def __missing__(self, key):
        self[key] = len(self)
        return self[key]


ROWS_ACROSS, ROWS_DIRECT = (3, -3), (2, -2, 1, -1)
COLS_ACROSS, COLS_DIRECT = (2, -2), (1, -1)
FIRST = (
    ("r", 1, 0), ("r", -3, 0), ("r", 3, 0), ("r", -2, 0), ("c", 2, 0), ("c", 1, 0),
    ("c", -2, 0), ("r", 0, 1), ("r", 2, 0), ("r", -1, 0), ("c", 0, 1), ("c", -1, 0),
)
EARLY = 9
ORDER = (
    "g", "mask", "sold0", ("r", 0, 1), "sold1", "sold2",
    "g1", ("c", 1, 0), ("c", -2, 0), ("r", 3, 0), ("c", 2, 0), ("c", -1, 0),
    ("r", -3, 0), ("c", 0, 1), "p1", "g2", ("c", -3, 0), ("r", 3, 1),
    ("c", -2, 1), ("c", 3, 0), ("c", 1, 1), ("c", -1, 1), ("r", -3, 1), ("c", 2, 1),
    "c4_0", "p2b", "turnA", "p2a", ("c", -3, 1), "g3",
    "c4_1", ("c", 3, 1), "turnB", "white0", "white1", "white2",
    "back2", "back1", "back0", "gramA0", "gramA1", "gramA2",
    "gramA3", "gramB0", "gs", "gramB1", "gramB2", "gramB3",
    "psum", "prod",
)


def kernel(
    rows_h, cols_h, w_h, mask_v, old_h, prob_h, new_o, prod_o,
    R, RT, C, W, Wm, WH, Y, OLD, PR, PB, PX, Q, QB, QR, QS, GX, GS, GZ, GF, ss, rs, ls,
):
    row, col = lax.axis_index("row"), lax.axis_index("col")
    core, y, xh = row % 2, (row // 2) % NY, row // (2 * NY)
    z, xl = col // 2, col % 2

    def at_z(k):
        return (z + k + NZ) % NZ

    def at_y(k):
        return (y + k + NY) % NY

    def to_z(k):
        return (row, at_z(k) * 2 + xl)

    def to_y(k):
        return ((xh * NY + at_y(k)) * 2 + core, col)

    other_row = ((1 - xh) * NY + y) * 2 + core
    to_xl = (row, z * 2 + 1 - xl)
    to_xh = (other_row, col)
    to_diagonal = (other_row, z * 2 + 1 - xl)
    to_core = ((xh * NY + y) * 2 + 1 - core, col)

    barrier = pltpu.get_barrier_semaphore()
    others = [to_z(k) for k in (1, -1, 2, -2, 3, -3)] + [to_y(k) for k in (1, -1, 2, -2)]
    others += [to_xl, to_xh, to_diagonal, to_core]
    for other in others:
        pl.semaphore_signal(barrier, inc=1, device_id=other, device_id_type=MESH)

    loads = {
        name: pltpu.make_async_copy(src, dst, ls.at[i])
        for i, (name, src, dst) in enumerate(
            (
                ("cols", cols_h, C.at[xh, y, core]),
                ("probes", prob_h, PR),
                ("rows", rows_h, R.at[z, xl]),
                ("whitening", w_h, W),
                ("old", old_h, OLD),
            )
        )
    }
    for load in loads.values():
        load.start()
    pl.semaphore_wait(barrier, len(others))

    sems, sent, seen = Names(), [], set()

    def send(src, dst, name, device):
        copy = pltpu.make_async_remote_copy(
            src_ref=src,
            dst_ref=dst,
            send_sem=ss.at[len(sent)],
            recv_sem=rs.at[sems[name]],
            device_id=device,
            device_id_type=MESH,
        )
        copy.start()
        sent.append(copy)

    def loaded(name):
        if name not in seen:
            seen.add(name)
            loads[name].wait()

    def place(name):
        kind, k, *side = name
        if kind == "r":
            at = (at_z(k), xl if side[0] == 0 else 1 - xl)
            return R.at[(*at, pl.ds(0 if k > 0 else 16, 16))] if abs(k) == 6 else R.at[at]
        if kind in ("c", "s"):
            at = (xh if side[0] == 0 else 1 - xh, at_y(k), core if kind == "c" else 1 - core)
            if kind == "c" and abs(k) == 4:
                return C.at[(*at, slice(None), pl.ds(0 if k > 0 else 512, 512))]
            return C.at[at]
        if kind == "gx":
            return GX.at[k]
        if kind in ("ga", "gb"):
            return GZ.at[{"ga": {-1: 0, 1: 1, 2: 2}, "gb": {4: 3, -4: 4}}[kind][k]]
        if kind == "gf":
            if abs(k) == 4:
                return GF.at[xh if k > 0 else 1 - xh, at_y(k), core]
            return GF.at[:, at_y(k), core]
        if kind == "gs":
            return GF.at[:, :, 1 - core]
        if kind == "px":
            return PX
        if kind == "qa":
            return QR.at[{4: 0, 5: 1, 6: 2, -4: 3, -5: 4}[k]]
        return QR.at[{1: 5, -1: 6, 2: 7, -2: 8, 3: 9, -3: 10}[k]]

    def need(name):
        if name not in seen:
            seen.add(name)
            ref = place(name)
            pltpu.make_async_remote_copy(
                src_ref=ref, dst_ref=ref, send_sem=ss.at[0], recv_sem=rs.at[sems[name]],
                device_id=to_core, device_id_type=MESH,
            ).wait_recv()

    def buf(kind, k, side):
        if kind == "r":
            return R.at[at_z(k), xl if side == 0 else 1 - xl]
        return C.at[xh if side == 0 else 1 - xh, at_y(k), core]

    def relay_rows(k, side):
        s = 1 if k > 0 else -1
        b = buf("r", k, side)
        half = b.at[pl.ds(0 if s > 0 else 16, 16)]
        send(half, half, ("r", 6 * s, side), to_z(-3 * s))
        send(b, b, ("r", 5 * s, side), to_z(-2 * s))
        send(b, b, ("r", 4 * s, side), to_z(-s))

    def relay_cols(k, side):
        s = 1 if k > 0 else -1
        b = buf("c", k, side)
        half = b.at[:, pl.ds(0 if s > 0 else 512, 512)]
        send(half, half, ("c", 4 * s, side), to_y(-2 * s))
        send(b, b, ("c", 3 * s, side), to_y(-s))

    def to_sibling(k, side):
        b = buf("c", k, side)
        send(b, b, ("s", k, side), to_core)

    def came(name):
        kind, k, side = name
        need(name)
        b = buf(kind, k, side)
        if kind == "r":
            if side == 0 and k in ROWS_ACROSS and abs(k) != 3:
                send(b, b, ("r", k, 1), to_xl)
            if abs(k) == 3:
                relay_rows(k, side)
                if side == 0 and k in ROWS_ACROSS:
                    send(b, b, ("r", k, 1), to_xl)
            if side == 1 and k == 0:
                for d in ROWS_DIRECT:
                    send(b, b, ("r", -d, 1), to_z(d))
        else:
            if side == 0 and k in COLS_ACROSS:
                send(b, b, ("c", k, 1), to_xh)
            if abs(k) == 2:
                relay_cols(k, side)
            if side == 1 and k == 0:
                for d in COLS_DIRECT:
                    send(b, b, ("c", -d, 1), to_y(d))
            to_sibling(k, side)

    def last_cols(side):
        need(("c", 4, side))
        need(("c", -4, side))
        to_sibling(4, side)

    def start(name):
        kind, k, side = name
        if kind == "c":
            device = to_xh if side else to_y(-k)
            send(cols_h, C.at[xh, y, core], name, device)
        else:
            device = to_xl if side else to_z(-k)
            send(rows_h, R.at[z, xl], name, device)

    for name in FIRST[:EARLY]:
        start(name)

    state = {}

    def g_share():
        loaded("cols")
        loaded("probes")
        phi, plo = split2(PR[...])
        state["phi"], state["both"] = phi, jnp.concatenate([phi, plo], axis=0)
        share = unpack(dot(C[xh, y, core], state["both"], ((1,), (1,))))
        state["mine"] = share
        GS[0, 0] = pack(share)
        for i, device in enumerate((to_xl, to_xh, to_diagonal)):
            send(GS.at[0, 0], GX.at[i], ("gx", i), device)
        for name in FIRST[EARLY:]:
            start(name)
        send(cols_h, C.at[xh, y, core], ("s", 0, 0), to_core)

    def g_x():
        for i in range(3):
            need(("gx", i))
        state["mine"] = state["mine"] + unpack(GX[0])
        state["theirs"] = unpack(GX[1]) + unpack(GX[2])
        GS[1, 0] = pack(state["mine"])
        GS[1, 1] = pack(state["theirs"])
        for k in (2, 1, -1):
            send(GS.at[1], place(("ga", k)), ("ga", k), to_z(-k))

    def g_add(names):
        for name in names:
            need(name)
            got = place(name)
            state["mine"] = state["mine"] + unpack(got[0])
            state["theirs"] = state["theirs"] + unpack(got[1])

    def g_z():
        g_add([("ga", k) for k in (1, -1, 2)])
        GS[2, 0] = pack(state["mine"])
        GS[2, 1] = pack(state["theirs"])
        for k in (4, -4):
            send(GS.at[2], place(("gb", k)), ("gb", k), to_z(-k))

    def g_y():
        g_add([("gb", k) for k in (4, -4)])
        GF[xh, y, core] = pack(state["mine"])
        GF[1 - xh, y, core] = pack(state["theirs"])
        for k in (1, -1, 2, -2):
            need(("c", k, 0))
        for k in (4, -4):
            b = GF.at[xh if k > 0 else 1 - xh, y, core]
            send(b, b, ("gf", k), to_y(-k))
        for k in (3, -3, 2, -2, 1, -1):
            send(GF.at[:, y, core], GF.at[:, y, core], ("gf", k), to_y(-k))

    def g_core():
        for k in (1, -1, 2, -2, 3, -3, 4, -4):
            need(("gf", k))
        send(GF.at[:, :, core], GF.at[:, :, core], ("gs", 0), to_core)

    def old_products(i):
        if i == 0:
            loaded("old")
        at = pl.ds(128 * i, 128)
        hi, lo = split2(OLD[at])
        PB[4 * i : 4 * i + 4] = pack(
            unpack(dot(hi, state["both"], ((1,), (1,)))) + dot(lo, state["phi"], ((1,), (1,)))
        ).reshape(4, 2, 16, 128)
        if i == 2:
            send(PB.at[:, 1 - xl], PX, ("px", 0), to_xl)

    def q_x():
        need(("px", 0))
        Q[...] = unpack(PB[:, xl]) + unpack(PX[...])
        QB[...] = pack(Q[...])
        for k in (6, 5, 4, -5, -4):
            s = 1 if k > 0 else -1
            send(QB.at[at_z(-k)], place(("qa", k)), ("qa", k), to_z(-(k - 3 * s)))
        for k in (2, -2, 1, -1):
            send(QB.at[at_z(-k)], place(("q", k)), ("q", k), to_z(-k))

    def q_far(s):
        total = Q[at_z(-3 * s)]
        for k in (4, 5, 6) if s > 0 else (-4, -5):
            need(("qa", k))
            total = total + unpack(place(("qa", k))[...])
        QS[0 if s > 0 else 1] = pack(total)
        send(QS.at[0 if s > 0 else 1], place(("q", 3 * s)), ("q", 3 * s), to_z(-3 * s))

    def q_sum():
        total = Q[z]
        for k in (1, -1, 2, -2, 3, -3):
            need(("q", k))
            total = total + unpack(place(("q", k))[...])
        state["old"] = total

    def mask():
        loaded("whitening")
        obs = lax.broadcasted_iota(jnp.int32, (768, 128), 0)
        first = COMP * lax.broadcasted_iota(jnp.int32, (768, 128), 1)
        keep = (obs >= first) & (obs < first + COMP)
        kept = jnp.sum(jnp.where(keep, mask_v[...].astype(F32), 0.0), axis=1, keepdims=True)
        Wm[...] = W[...] * kept.astype(BF)

    def turn(js):
        loaded("rows")
        reach = (1, -1, 2, -2, 3, -3) if 0 in js else (4, -4, 5, -5, 6, -6)
        for side in (0, 1):
            for k in reach:
                need(("r", k, side))
        need(("r", 0, 1))
        for j in js:
            pair = (z // 2 + j + 6) % 6
            block = R[pl.ds(2 * pair, 2)].reshape(128, 384)
            RT[:, pl.ds(pl.multiple_of(128 * pair, 128), 128)] = block.T

    def whiten(b):
        at, end = slice(256 * b, 256 * b + 256), 256 * b + 256
        WH[:, at] = dot(RT[:, :end], W[at, :end], ((1,), (1,))).astype(BF)

    def back(b):
        at = slice(256 * b, 256 * b + 256)
        hi, lo = split2(dot(WH[:, 256 * b :], Wm[256 * b :, at]))
        Y[:384, at] = hi
        Y[384:, at] = lo

    def gram(side, n):
        for k in (0, 1, -1, 2, -2, 3, -3, 4):
            need(("s", k, side))
        h = xh if side == 0 else 1 - xh
        at = pl.ds(256 * n, 256)
        left = Y[:, pl.ds(pl.multiple_of(384 * h, 128), 384)]
        both = dot(left, C[h, :, :, :, at].reshape(384, 256))
        new = OLD if side == 0 else new_o
        new[:, at] = OLD[:, at] + (both[:384] + both[384:])

    def products():
        need(("gs", 0))
        total = state["old"]
        at = pl.multiple_of(col * 16, 16)
        for first in (0, 384):
            total = total + unpack(dot(Y[pl.ds(first + at, 16), :], GF[...].reshape(768, 128)))
        prod_o[...] = total

    tasks = dict(
        g=g_share, g1=g_x, g2=g_z, g3=g_y, gs=g_core, p1=q_x, psum=q_sum, mask=mask, prod=products,
        c4_0=lambda: last_cols(0), c4_1=lambda: last_cols(1), p2a=lambda: q_far(1), p2b=lambda: q_far(-1),
        turnA=lambda: turn((0, 1, -1)), turnB=lambda: turn((2, -2, 3)),
    )
    for step in ORDER:
        if step in tasks:
            tasks[step]()
        elif isinstance(step, str):
            what, i = step[:-1], int(step[-1])
            many = dict(sold=old_products, white=whiten, back=back)
            if what in many:
                many[what](i)
            else:
                gram(0 if what == "gramA" else 1, i)
        else:
            came(step)
    for copy in sent:
        copy.wait_send()


def write_out(new_v, prod_v, new_h, prod_h, sems):
    copies = [pltpu.make_async_copy(prod_v, prod_h, sems.at[4])]
    for i in range(4):
        rows = pl.ds(96 * i, 96)
        copies.append(pltpu.make_async_copy(new_v.at[rows], new_h.at[rows], sems.at[i]))
    for copy in copies:
        copy.start()
    for copy in copies:
        copy.wait()


def body(design_rows, design_cols, whitening, epoch_mask, normal_old, probes):
    vmem = pl.BlockSpec(memory_space=pltpu.VMEM)
    hbm = pl.BlockSpec(memory_space=pltpu.HBM)
    new, products = pl.pallas_call(
        kernel,
        out_shape=(pltpu.VMEM((384, 1024), F32), pltpu.VMEM((16, 64), F32)),
        in_specs=[hbm, hbm, hbm, vmem, hbm, hbm],
        out_specs=(vmem, vmem),
        scratch_shapes=[
            pltpu.VMEM((NZ, 2, 32, 384), BF),
            pltpu.VMEM((384, 768), BF),
            pltpu.VMEM((2, NY, 2, 24, 1024), BF),
            pltpu.VMEM((768, 768), BF),
            pltpu.VMEM((768, 768), BF),
            pltpu.VMEM((384, 768), BF),
            pltpu.VMEM((768, 768), BF),
            pltpu.VMEM((384, 1024), F32),
            pltpu.VMEM((64, 1024), F32),
            pltpu.VMEM((NZ, 2, 16, 128), BF),
            pltpu.VMEM((NZ, 16, 128), BF),
            pltpu.VMEM((NZ, 16, 64), F32),
            pltpu.VMEM((NZ, 16, 128), BF),
            pltpu.VMEM((11, 16, 128), BF),
            pltpu.VMEM((2, 16, 128), BF),
            pltpu.VMEM((3, 24, 128), BF),
            pltpu.VMEM((3, 2, 24, 128), BF),
            pltpu.VMEM((5, 2, 24, 128), BF),
            pltpu.VMEM((2, NY, 2, 24, 128), BF),
            pltpu.SemaphoreType.DMA((128,)),
            pltpu.SemaphoreType.DMA((128,)),
            pltpu.SemaphoreType.DMA((5,)),
        ],
        compiler_params=pltpu.CompilerParams(
            collective_id=0, has_side_effects=True, vmem_limit_bytes=56 * 2**20
        ),
        name="normal_update",
    )(
        design_rows,
        design_cols,
        whitening,
        epoch_mask.reshape(1, 128),
        normal_old,
        probes.T,
    )
    return pl.pallas_call(
        write_out,
        out_shape=(
            jax.ShapeDtypeStruct((384, 1024), F32),
            jax.ShapeDtypeStruct((16, 64), F32),
        ),
        in_specs=[vmem, vmem],
        out_specs=(hbm, hbm),
        scratch_shapes=[pltpu.SemaphoreType.DMA((5,))],
        compiler_params=pltpu.CompilerParams(vmem_limit_bytes=4 * 2**20),
        name="write_out",
    )(new, products)


def solution(mesh):
    placed = (P("col", "row"), P("row", "col"), P(), P(), P("row", "col"), P("col", None))
    return jax.shard_map(
        body,
        mesh=mesh,
        in_specs=placed,
        out_specs=(P("row", "col"), P(("row", "col"), None)),
        check_vma=False,
    )
```

```python
import jax
import jax.numpy as jnp
from jax import lax
from jax.experimental import pallas as pl
from jax.experimental.pallas import tpu as pltpu
from jax.sharding import PartitionSpec as P

MESH = pl.DeviceIdType.MESH
COMP = 6
NZ, NY = 12, 8
BF, F32 = jnp.bfloat16, jnp.float32


def split2(x):
    hi = x.astype(BF)
    return hi, (x - hi.astype(F32)).astype(BF)


def dot(a, b, dims=((1,), (0,))):
    return lax.dot_general(a, b, (dims, ((), ())), preferred_element_type=F32)


def pack(x):
    return jnp.concatenate(split2(x), axis=-1)


def unpack(x):
    x = x.astype(F32)
    return x[..., :64] + x[..., 64:]


class Names(dict):
    def __missing__(self, key):
        self[key] = len(self)
        return self[key]


ROWS_ACROSS, ROWS_DIRECT = (3, -3), (2, -2, 1, -1)
COLS_ACROSS, COLS_DIRECT = (2, -2), (1, -1)
FIRST = (
    ("r", 1, 0), ("r", -3, 0), ("r", 3, 0), ("r", -2, 0), ("c", 2, 0), ("c", 1, 0),
    ("c", -2, 0), ("r", 0, 1), ("r", 2, 0), ("r", -1, 0), ("c", 0, 1), ("c", -1, 0),
)
EARLY = 9
ORDER = (
    "g", "mask", "sold0", ("r", 0, 1), "sold1", "sold2",
    "g1", ("c", 1, 0), ("c", -2, 0), ("r", 3, 0), ("c", 2, 0), ("c", -1, 0),
    ("r", -3, 0), ("c", 0, 1), "p1", "g2", ("c", -3, 0), ("r", 3, 1),
    ("c", -2, 1), ("c", 3, 0), ("c", 1, 1), ("c", -1, 1), ("r", -3, 1), ("c", 2, 1),
    "c4_0", "p2b", "turnA", "p2a", ("c", -3, 1), "g3",
    "c4_1", ("c", 3, 1), "turnB", "white0", "white1", "white2",
    "back2", "back1", "back0", "gramA0", "gramA1", "gramA2",
    "gramA3", "gramB0", "gs", "gramB1", "gramB2", "gramB3",
    "psum", "prod",
)


def kernel(
    rows_h, cols_h, w_h, mask_h, old_h, prob_h, new_o, prod_o,
    R, RT, C, W, Wm, WH, Y, OLD, PR, PB, PX, Q, QB, QR, QS, GX, GS, GZ, GF, MASK, ss, rs, ls,
):
    row, col = lax.axis_index("row"), lax.axis_index("col")
    core, y, xh = row % 2, (row // 2) % NY, row // (2 * NY)
    z, xl = col // 2, col % 2

    def at_z(k):
        return (z + k + NZ) % NZ

    def at_y(k):
        return (y + k + NY) % NY

    def to_z(k):
        return (row, at_z(k) * 2 + xl)

    def to_y(k):
        return ((xh * NY + at_y(k)) * 2 + core, col)

    other_row = ((1 - xh) * NY + y) * 2 + core
    to_xl = (row, z * 2 + 1 - xl)
    to_xh = (other_row, col)
    to_diagonal = (other_row, z * 2 + 1 - xl)
    to_core = ((xh * NY + y) * 2 + 1 - core, col)

    barrier = pltpu.get_barrier_semaphore()
    others = [to_z(k) for k in (1, -1, 2, -2, 3, -3)] + [to_y(k) for k in (1, -1, 2, -2)]
    others += [to_xl, to_xh, to_diagonal, to_core]
    for other in others:
        pl.semaphore_signal(barrier, inc=1, device_id=other, device_id_type=MESH)

    loads = {
        name: pltpu.make_async_copy(src, dst, ls.at[i])
        for i, (name, src, dst) in enumerate(
            (
                ("cols", cols_h, C.at[xh, y, core]),
                ("probes", prob_h, PR),
                ("rows", rows_h, R.at[z, xl]),
                ("mask", mask_h, MASK),
                ("whitening", w_h, W),
                ("old", old_h, OLD),
            )
        )
    }
    for load in loads.values():
        load.start()

    sems, sent, seen, state = Names(), [], set(), {}

    def loaded(name):
        if name not in seen:
            seen.add(name)
            loads[name].wait()

    loaded("cols")
    loaded("probes")
    phi, plo = split2(PR[...])
    state["phi"], state["both"] = phi, jnp.concatenate([phi, plo], axis=0)
    state["mine"] = unpack(dot(C[xh, y, core], state["both"], ((1,), (1,))))
    GS[0, 0] = pack(state["mine"])

    def mask():
        loaded("mask")
        loaded("whitening")
        obs = lax.broadcasted_iota(jnp.int32, (768, 128), 0)
        first = COMP * lax.broadcasted_iota(jnp.int32, (768, 128), 1)
        keep = (obs >= first) & (obs < first + COMP)
        kept = jnp.sum(jnp.where(keep, MASK[...].astype(F32), 0.0), axis=1, keepdims=True)
        Wm[...] = W[...] * kept.astype(BF)

    pl.semaphore_wait(barrier, len(others))

    def send(src, dst, name, device):
        copy = pltpu.make_async_remote_copy(
            src_ref=src,
            dst_ref=dst,
            send_sem=ss.at[len(sent)],
            recv_sem=rs.at[sems[name]],
            device_id=device,
            device_id_type=MESH,
        )
        copy.start(priority=0)
        sent.append(copy)

    def place(name):
        kind, k, *side = name
        if kind == "r":
            at = (at_z(k), xl if side[0] == 0 else 1 - xl)
            return R.at[(*at, pl.ds(0 if k > 0 else 16, 16))] if abs(k) == 6 else R.at[at]
        if kind in ("c", "s"):
            at = (xh if side[0] == 0 else 1 - xh, at_y(k), core if kind == "c" else 1 - core)
            if kind == "c" and abs(k) == 4:
                return C.at[(*at, slice(None), pl.ds(0 if k > 0 else 512, 512))]
            return C.at[at]
        if kind == "gx":
            return GX.at[k]
        if kind in ("ga", "gb"):
            return GZ.at[{"ga": {-1: 0, 1: 1, 2: 2}, "gb": {4: 3, -4: 4}}[kind][k]]
        if kind == "gf":
            if abs(k) == 4:
                return GF.at[xh if k > 0 else 1 - xh, at_y(k), core]
            return GF.at[:, at_y(k), core]
        if kind == "gs":
            return GF.at[:, at_y(k), 1 - core]
        if kind == "px":
            return PX
        if kind == "qa":
            return QR.at[{4: 0, 5: 1, 6: 2, -4: 3, -5: 4}[k]]
        return QR.at[{1: 5, -1: 6, 2: 7, -2: 8, 3: 9, -3: 10}[k]]

    def need(name):
        if name not in seen:
            seen.add(name)
            ref = place(name)
            pltpu.make_async_remote_copy(
                src_ref=ref, dst_ref=ref, send_sem=ss.at[0], recv_sem=rs.at[sems[name]],
                device_id=to_core, device_id_type=MESH,
            ).wait_recv()

    def buf(kind, k, side):
        if kind == "r":
            return R.at[at_z(k), xl if side == 0 else 1 - xl]
        return C.at[xh if side == 0 else 1 - xh, at_y(k), core]

    def relay_rows(k, side):
        s = 1 if k > 0 else -1
        b = buf("r", k, side)
        half = b.at[pl.ds(0 if s > 0 else 16, 16)]
        send(half, half, ("r", 6 * s, side), to_z(-3 * s))
        send(b, b, ("r", 5 * s, side), to_z(-2 * s))
        send(b, b, ("r", 4 * s, side), to_z(-s))

    def relay_cols(k, side):
        s = 1 if k > 0 else -1
        b = buf("c", k, side)
        half = b.at[:, pl.ds(0 if s > 0 else 512, 512)]
        send(half, half, ("c", 4 * s, side), to_y(-2 * s))
        send(b, b, ("c", 3 * s, side), to_y(-s))

    def to_sibling(k, side):
        b = buf("c", k, side)
        send(b, b, ("s", k, side), to_core)

    def came(name):
        kind, k, side = name
        need(name)
        b = buf(kind, k, side)
        if kind == "r":
            if side == 0 and k in ROWS_ACROSS and abs(k) != 3:
                send(b, b, ("r", k, 1), to_xl)
            if abs(k) == 3:
                relay_rows(k, side)
                if side == 0 and k in ROWS_ACROSS:
                    send(b, b, ("r", k, 1), to_xl)
            if side == 1 and k == 0:
                for d in ROWS_DIRECT:
                    send(b, b, ("r", -d, 1), to_z(d))
        else:
            if side == 0 and k in COLS_ACROSS:
                send(b, b, ("c", k, 1), to_xh)
            if abs(k) == 2:
                relay_cols(k, side)
            if side == 1 and k == 0:
                for d in COLS_DIRECT:
                    send(b, b, ("c", -d, 1), to_y(d))
            to_sibling(k, side)

    def last_cols(side):
        need(("c", 4, side))
        need(("c", -4, side))
        to_sibling(4, side)

    def start(name):
        kind, k, side = name
        if kind == "c":
            device = to_xh if side else to_y(-k)
            send(cols_h, C.at[xh, y, core], name, device)
        else:
            device = to_xl if side else to_z(-k)
            send(rows_h, R.at[z, xl], name, device)

    for name in FIRST[:EARLY]:
        start(name)

    def g_share():
        for i, device in enumerate((to_xl, to_xh, to_diagonal)):
            send(GS.at[0, 0], GX.at[i], ("gx", i), device)
        for name in FIRST[EARLY:]:
            start(name)
        send(cols_h, C.at[xh, y, core], ("s", 0, 0), to_core)

    def g_x():
        for i in range(3):
            need(("gx", i))
        state["mine"] = state["mine"] + unpack(GX[0])
        state["theirs"] = unpack(GX[1]) + unpack(GX[2])
        GS[1, 0] = pack(state["mine"])
        GS[1, 1] = pack(state["theirs"])
        for k in (2, 1, -1):
            send(GS.at[1], place(("ga", k)), ("ga", k), to_z(-k))

    def g_add(names):
        for name in names:
            need(name)
            got = place(name)
            state["mine"] = state["mine"] + unpack(got[0])
            state["theirs"] = state["theirs"] + unpack(got[1])

    def g_z():
        g_add([("ga", k) for k in (1, -1, 2)])
        GS[2, 0] = pack(state["mine"])
        GS[2, 1] = pack(state["theirs"])
        for k in (4, -4):
            send(GS.at[2], place(("gb", k)), ("gb", k), to_z(-k))

    def g_y():
        g_add([("gb", k) for k in (4, -4)])
        GF[xh, y, core] = pack(state["mine"])
        GF[1 - xh, y, core] = pack(state["theirs"])
        for k in (1, -1, 2, -2):
            need(("c", k, 0))
        for k in (4, -4):
            b = GF.at[xh if k > 0 else 1 - xh, y, core]
            send(b, b, ("gf", k), to_y(-k))
        for k in (3, -3, 2, -2, 1, -1):
            send(GF.at[:, y, core], GF.at[:, y, core], ("gf", k), to_y(-k))

    def g_core():
        for k in (0, 1, -1, 2, -2, 3, -3, 4):
            if k:
                need(("gf", k))
            if k == 4:
                need(("gf", -4))
            b = GF.at[:, at_y(k), core]
            send(b, b, ("gs", k), to_core)

    def old_products(i):
        if i == 0:
            loaded("old")
        at = pl.ds(128 * i, 128)
        hi, lo = split2(OLD[at])
        PB[4 * i : 4 * i + 4] = pack(
            unpack(dot(hi, state["both"], ((1,), (1,)))) + dot(lo, state["phi"], ((1,), (1,)))
        ).reshape(4, 2, 16, 128)
        if i == 2:
            send(PB.at[:, 1 - xl], PX, ("px", 0), to_xl)

    def q_x():
        need(("px", 0))
        Q[...] = unpack(PB[:, xl]) + unpack(PX[...])
        QB[...] = pack(Q[...])
        for k in (6, 5, 4, -5, -4):
            s = 1 if k > 0 else -1
            send(QB.at[at_z(-k)], place(("qa", k)), ("qa", k), to_z(-(k - 3 * s)))
        for k in (2, -2, 1, -1):
            send(QB.at[at_z(-k)], place(("q", k)), ("q", k), to_z(-k))

    def q_far(s):
        total = Q[at_z(-3 * s)]
        for k in (4, 5, 6) if s > 0 else (-4, -5):
            need(("qa", k))
            total = total + unpack(place(("qa", k))[...])
        QS[0 if s > 0 else 1] = pack(total)
        send(QS.at[0 if s > 0 else 1], place(("q", 3 * s)), ("q", 3 * s), to_z(-3 * s))

    def q_sum():
        total = Q[z]
        for k in (1, -1, 2, -2, 3, -3):
            need(("q", k))
            total = total + unpack(place(("q", k))[...])
        state["old"] = total

    def turn(js):
        loaded("rows")
        reach = (1, -1, 2, -2, 3, -3) if 0 in js else (4, -4, 5, -5, 6, -6)
        for side in (0, 1):
            for k in reach:
                need(("r", k, side))
        need(("r", 0, 1))
        for j in js:
            pair = (z // 2 + j + 6) % 6
            block = R[pl.ds(2 * pair, 2)].reshape(128, 384)
            RT[:, pl.ds(pl.multiple_of(128 * pair, 128), 128)] = block.T

    def whiten(b):
        at, end = slice(256 * b, 256 * b + 256), 256 * b + 256
        WH[:, at] = dot(RT[:, :end], W[at, :end], ((1,), (1,))).astype(BF)

    def back(b):
        at = slice(256 * b, 256 * b + 256)
        hi, lo = split2(dot(WH[:, 256 * b :], Wm[256 * b :, at]))
        Y[:384, at] = hi
        Y[384:, at] = lo

    def gram(side, n):
        for k in (0, 1, -1, 2, -2, 3, -3, 4):
            need(("s", k, side))
        h = xh if side == 0 else 1 - xh
        at = pl.ds(256 * n, 256)
        left = Y[:, pl.ds(pl.multiple_of(384 * h, 128), 384)]
        both = dot(left, C[h, :, :, :, at].reshape(384, 256))
        new = OLD if side == 0 else new_o
        new[:, at] = OLD[:, at] + (both[:384] + both[384:])

    def products():
        for k in (0, 1, -1, 2, -2, 3, -3, 4):
            need(("gs", k))
        total = state["old"]
        at = pl.multiple_of(col * 16, 16)
        for first in (0, 384):
            total = total + unpack(dot(Y[pl.ds(first + at, 16), :], GF[...].reshape(768, 128)))
        prod_o[...] = total

    tasks = dict(
        g=g_share, g1=g_x, g2=g_z, g3=g_y, gs=g_core, p1=q_x, psum=q_sum, mask=mask, prod=products,
        c4_0=lambda: last_cols(0), c4_1=lambda: last_cols(1), p2a=lambda: q_far(1), p2b=lambda: q_far(-1),
        turnA=lambda: turn((0, 1, -1)), turnB=lambda: turn((2, -2, 3)),
    )
    for step in ORDER:
        if step in tasks:
            tasks[step]()
        elif isinstance(step, str):
            what, i = step[:-1], int(step[-1])
            many = dict(sold=old_products, white=whiten, back=back)
            if what in many:
                many[what](i)
            else:
                gram(0 if what == "gramA" else 1, i)
        else:
            came(step)
    for copy in sent:
        copy.wait_send()


def write_out(new_v, prod_v, new_h, prod_h, sems):
    copies = [pltpu.make_async_copy(prod_v, prod_h, sems.at[4])]
    for i in range(4):
        rows = pl.ds(96 * i, 96)
        copies.append(pltpu.make_async_copy(new_v.at[rows], new_h.at[rows], sems.at[i]))
    for copy in copies:
        copy.start()
    for copy in copies:
        copy.wait()


def body(design_rows, design_cols, whitening, epoch_mask, normal_old, probes):
    vmem = pl.BlockSpec(memory_space=pltpu.VMEM)
    hbm = pl.BlockSpec(memory_space=pltpu.HBM)
    new, products = pl.pallas_call(
        kernel,
        out_shape=(pltpu.VMEM((384, 1024), F32), pltpu.VMEM((16, 64), F32)),
        in_specs=[hbm] * 6,
        out_specs=(vmem, vmem),
        scratch_shapes=[
            pltpu.VMEM((NZ, 2, 32, 384), BF),
            pltpu.VMEM((384, 768), BF),
            pltpu.VMEM((2, NY, 2, 24, 1024), BF),
            pltpu.VMEM((768, 768), BF),
            pltpu.VMEM((768, 768), BF),
            pltpu.VMEM((384, 768), BF),
            pltpu.VMEM((768, 768), BF),
            pltpu.VMEM((384, 1024), F32),
            pltpu.VMEM((64, 1024), F32),
            pltpu.VMEM((NZ, 2, 16, 128), BF),
            pltpu.VMEM((NZ, 16, 128), BF),
            pltpu.VMEM((NZ, 16, 64), F32),
            pltpu.VMEM((NZ, 16, 128), BF),
            pltpu.VMEM((11, 16, 128), BF),
            pltpu.VMEM((2, 16, 128), BF),
            pltpu.VMEM((3, 24, 128), BF),
            pltpu.VMEM((3, 2, 24, 128), BF),
            pltpu.VMEM((5, 2, 24, 128), BF),
            pltpu.VMEM((2, NY, 2, 24, 128), BF),
            pltpu.VMEM((1, 128), jnp.int32),
            pltpu.SemaphoreType.DMA((128,)),
            pltpu.SemaphoreType.DMA((128,)),
            pltpu.SemaphoreType.DMA((6,)),
        ],
        compiler_params=pltpu.CompilerParams(
            collective_id=0, has_side_effects=True, vmem_limit_bytes=56 * 2**20
        ),
        name="normal_update",
    )(
        design_rows,
        design_cols,
        whitening,
        epoch_mask.reshape(1, 128),
        normal_old,
        probes.T,
    )
    return pl.pallas_call(
        write_out,
        out_shape=(
            jax.ShapeDtypeStruct((384, 1024), F32),
            jax.ShapeDtypeStruct((16, 64), F32),
        ),
        in_specs=[vmem, vmem],
        out_specs=(hbm, hbm),
        scratch_shapes=[pltpu.SemaphoreType.DMA((5,))],
        compiler_params=pltpu.CompilerParams(vmem_limit_bytes=4 * 2**20),
        name="write_out",
    )(new, products)


def solution(mesh):
    placed = (P("col", "row"), P("row", "col"), P(), P(), P("row", "col"), P("col", None))
    return jax.shard_map(
        body,
        mesh=mesh,
        in_specs=placed,
        out_specs=(P("row", "col"), P(("row", "col"), None)),
        check_vma=False,
    )
```

```python
import jax
import jax.numpy as jnp
from jax import lax
from jax.experimental import pallas as pl
from jax.experimental.pallas import tpu as pltpu
from jax.sharding import PartitionSpec as P

MESH = pl.DeviceIdType.MESH
COMP = 6
NZ, NY = 12, 8
BF, F32 = jnp.bfloat16, jnp.float32


def split2(x):
    hi = x.astype(BF)
    return hi, (x - hi.astype(F32)).astype(BF)


def dot(a, b, dims=((1,), (0,))):
    return lax.dot_general(a, b, (dims, ((), ())), preferred_element_type=F32)


def pack(x):
    return jnp.concatenate(split2(x), axis=-1)


def unpack(x):
    x = x.astype(F32)
    return x[..., :64] + x[..., 64:]


class Names(dict):
    def __missing__(self, key):
        self[key] = len(self)
        return self[key]


ROWS_ACROSS, ROWS_DIRECT = (3, -3), (2, -2, 1, -1)
COLS_ACROSS, COLS_DIRECT = (2, -2, 1, -1), ()
FIRST = (
    ("c", -1, 0), ("r", 3, 0), ("r", -3, 0), ("r", 1, 0), ("c", 1, 0), ("r", 2, 0),
    ("r", 0, 1), ("c", -2, 0), ("r", -2, 0), ("c", 2, 0), ("c", 0, 1), ("r", -1, 0),
)
EARLY = 10
ORDER = (
    "g", "mask", "sold0", ("c", -1, 0), ("r", 0, 1), ("c", 1, 0),
    "sold1", "sold2", "g1", ("c", -2, 0), ("c", 2, 0), ("r", 3, 0),
    ("r", -3, 0), "g2", ("c", 0, 1), ("c", 1, 1), ("c", -1, 1), "p1",
    ("c", -3, 0), "c4_0", ("c", 3, 0), ("c", -2, 1), ("r", 3, 1), ("c", 2, 1),
    ("r", -3, 1), "turnA", "p2b", "p2a", "g3", ("c", -3, 1),
    ("c", 3, 1), "c4_1", "turnB", "white0", "white1", "white2",
    "back2", "back1", "back0", "gs", "gram0", "gram1",
    "gram2", "gram3", "psum", "prod",
)


def kernel(
    rows_h, cols_h, w_h, mask_h, old_h, prob_h, new_o, prod_o,
    R, RT, C, W, Wm, WH, Y, OLD, PR, PB, PX, Q, QB, QR, QS, GX, GS, GZ, GF, MASK, ss, rs, ls,
):
    row, col = lax.axis_index("row"), lax.axis_index("col")
    core, y, xh = row % 2, (row // 2) % NY, row // (2 * NY)
    z, xl = col // 2, col % 2

    def at_z(k):
        return (z + k + NZ) % NZ

    def at_y(k):
        return (y + k + NY) % NY

    def to_z(k):
        return (row, at_z(k) * 2 + xl)

    def to_y(k):
        return ((xh * NY + at_y(k)) * 2 + core, col)

    other_row = ((1 - xh) * NY + y) * 2 + core
    to_xl = (row, z * 2 + 1 - xl)
    to_xh = (other_row, col)
    to_diagonal = (other_row, z * 2 + 1 - xl)
    to_core = ((xh * NY + y) * 2 + 1 - core, col)

    barrier = pltpu.get_barrier_semaphore()
    others = [to_z(k) for k in (1, -1, 2, -2, 3, -3)] + [to_y(k) for k in (1, -1, 2, -2)]
    others += [to_xl, to_xh, to_diagonal, to_core]
    for other in others:
        pl.semaphore_signal(barrier, inc=1, device_id=other, device_id_type=MESH)

    loads = {
        name: pltpu.make_async_copy(src, dst, ls.at[i])
        for i, (name, src, dst) in enumerate(
            (
                ("cols", cols_h, C.at[xh, y, core]),
                ("probes", prob_h, PR),
                ("rows", rows_h, R.at[z, xl]),
                ("mask", mask_h, MASK),
                ("whitening", w_h, W),
                ("old", old_h, OLD),
            )
        )
    }
    for load in loads.values():
        load.start()

    sems, sent, seen, state = Names(), [], set(), {}

    def loaded(name):
        if name not in seen:
            seen.add(name)
            loads[name].wait()

    loaded("cols")
    loaded("probes")
    phi, plo = split2(PR[...])
    state["phi"], state["both"] = phi, jnp.concatenate([phi, plo], axis=0)
    state["mine"] = unpack(dot(C[xh, y, core], state["both"], ((1,), (1,))))
    GS[0, 0] = pack(state["mine"])

    def mask():
        loaded("mask")
        loaded("whitening")
        obs = lax.broadcasted_iota(jnp.int32, (768, 128), 0)
        first = COMP * lax.broadcasted_iota(jnp.int32, (768, 128), 1)
        keep = (obs >= first) & (obs < first + COMP)
        kept = jnp.sum(jnp.where(keep, MASK[...].astype(F32), 0.0), axis=1, keepdims=True)
        Wm[...] = W[...] * kept.astype(BF)

    pl.semaphore_wait(barrier, len(others))

    def send(src, dst, name, device):
        copy = pltpu.make_async_remote_copy(
            src_ref=src,
            dst_ref=dst,
            send_sem=ss.at[len(sent)],
            recv_sem=rs.at[sems[name]],
            device_id=device,
            device_id_type=MESH,
        )
        copy.start(priority=0)
        sent.append(copy)

    def place(name):
        kind, k, *side = name
        if kind == "r":
            at = (at_z(k), xl if side[0] == 0 else 1 - xl)
            return R.at[(*at, pl.ds(0 if k > 0 else 16, 16))] if abs(k) == 6 else R.at[at]
        if kind in ("c", "s"):
            at = (xh if side[0] == 0 else 1 - xh, at_y(k), core if kind == "c" else 1 - core)
            if kind == "c" and abs(k) == 4:
                return C.at[(*at, slice(None), pl.ds(0 if k > 0 else 512, 512))]
            return C.at[at]
        if kind == "gx":
            return GX.at[k]
        if kind in ("ga", "gb"):
            return GZ.at[{"ga": {-1: 0, 1: 1, 2: 2}, "gb": {4: 3, -4: 4}}[kind][k]]
        if kind == "gf":
            if abs(k) == 4:
                return GF.at[xh if k > 0 else 1 - xh, at_y(k), core]
            return GF.at[:, at_y(k), core]
        if kind == "gs":
            return GF.at[:, at_y(k), 1 - core]
        if kind == "px":
            return PX
        if kind == "qa":
            return QR.at[{4: 0, 5: 1, 6: 2, -4: 3, -5: 4}[k]]
        return QR.at[{1: 5, -1: 6, 2: 7, -2: 8, 3: 9, -3: 10}[k]]

    def need(name):
        if name not in seen:
            seen.add(name)
            ref = place(name)
            pltpu.make_async_remote_copy(
                src_ref=ref, dst_ref=ref, send_sem=ss.at[0], recv_sem=rs.at[sems[name]],
                device_id=to_core, device_id_type=MESH,
            ).wait_recv()

    def buf(kind, k, side):
        if kind == "r":
            return R.at[at_z(k), xl if side == 0 else 1 - xl]
        return C.at[xh if side == 0 else 1 - xh, at_y(k), core]

    def relay_rows(k, side):
        s = 1 if k > 0 else -1
        b = buf("r", k, side)
        half = b.at[pl.ds(0 if s > 0 else 16, 16)]
        send(half, half, ("r", 6 * s, side), to_z(-3 * s))
        send(b, b, ("r", 5 * s, side), to_z(-2 * s))
        send(b, b, ("r", 4 * s, side), to_z(-s))

    def relay_cols(k, side):
        s = 1 if k > 0 else -1
        b = buf("c", k, side)
        half = b.at[:, pl.ds(0 if s > 0 else 512, 512)]
        send(half, half, ("c", 4 * s, side), to_y(-2 * s))
        send(b, b, ("c", 3 * s, side), to_y(-s))

    def to_sibling(k, side):
        b = buf("c", k, side)
        send(b, b, ("s", k, side), to_core)

    def came(name):
        kind, k, side = name
        need(name)
        b = buf(kind, k, side)
        if kind == "r":
            if side == 0 and k in ROWS_ACROSS and abs(k) != 3:
                send(b, b, ("r", k, 1), to_xl)
            if abs(k) == 3:
                relay_rows(k, side)
                if side == 0 and k in ROWS_ACROSS:
                    send(b, b, ("r", k, 1), to_xl)
            if side == 1 and k == 0:
                for d in ROWS_DIRECT:
                    send(b, b, ("r", -d, 1), to_z(d))
        else:
            if side == 0 and k in COLS_ACROSS:
                send(b, b, ("c", k, 1), to_xh)
            if abs(k) == 2:
                relay_cols(k, side)
            if side == 1 and k == 0:
                for d in COLS_DIRECT:
                    send(b, b, ("c", -d, 1), to_y(d))
            to_sibling(k, side)

    def last_cols(side):
        need(("c", 4, side))
        need(("c", -4, side))
        to_sibling(4, side)

    def start(name):
        kind, k, side = name
        if kind == "c":
            device = to_xh if side else to_y(-k)
            send(cols_h, C.at[xh, y, core], name, device)
        else:
            device = to_xl if side else to_z(-k)
            send(rows_h, R.at[z, xl], name, device)

    for name in FIRST[:EARLY]:
        start(name)

    def g_share():
        for i, device in enumerate((to_xl, to_xh, to_diagonal)):
            send(GS.at[0, 0], GX.at[i], ("gx", i), device)
        for name in FIRST[EARLY:]:
            start(name)
        send(cols_h, C.at[xh, y, core], ("s", 0, 0), to_core)

    def g_x():
        for i in range(3):
            need(("gx", i))
        state["mine"] = state["mine"] + unpack(GX[0])
        state["theirs"] = unpack(GX[1]) + unpack(GX[2])
        GS[1, 0] = pack(state["mine"])
        GS[1, 1] = pack(state["theirs"])
        for k in (2, 1, -1):
            send(GS.at[1], place(("ga", k)), ("ga", k), to_z(-k))

    def g_add(names):
        for name in names:
            need(name)
            got = place(name)
            state["mine"] = state["mine"] + unpack(got[0])
            state["theirs"] = state["theirs"] + unpack(got[1])

    def g_z():
        g_add([("ga", k) for k in (1, -1, 2)])
        GS[2, 0] = pack(state["mine"])
        GS[2, 1] = pack(state["theirs"])
        for k in (4, -4):
            send(GS.at[2], place(("gb", k)), ("gb", k), to_z(-k))

    def g_y():
        g_add([("gb", k) for k in (4, -4)])
        GF[xh, y, core] = pack(state["mine"])
        GF[1 - xh, y, core] = pack(state["theirs"])
        for k in (1, -1, 2, -2):
            need(("c", k, 0))
        for k in (4, -4):
            b = GF.at[xh if k > 0 else 1 - xh, y, core]
            send(b, b, ("gf", k), to_y(-k))
        for k in (3, -3, 2, -2, 1, -1):
            send(GF.at[:, y, core], GF.at[:, y, core], ("gf", k), to_y(-k))

    def g_core():
        for k in (0, 1, -1, 2, -2, 3, -3, 4):
            if k:
                need(("gf", k))
            if k == 4:
                need(("gf", -4))
            b = GF.at[:, at_y(k), core]
            send(b, b, ("gs", k), to_core)

    def old_products(i):
        if i == 0:
            loaded("old")
        at = pl.ds(128 * i, 128)
        hi, lo = split2(OLD[at])
        PB[4 * i : 4 * i + 4] = pack(
            unpack(dot(hi, state["both"], ((1,), (1,)))) + dot(lo, state["phi"], ((1,), (1,)))
        ).reshape(4, 2, 16, 128)
        if i == 2:
            send(PB.at[:, 1 - xl], PX, ("px", 0), to_xl)

    def q_x():
        need(("px", 0))
        Q[...] = unpack(PB[:, xl]) + unpack(PX[...])
        QB[...] = pack(Q[...])
        for k in (6, 5, 4, -5, -4):
            s = 1 if k > 0 else -1
            send(QB.at[at_z(-k)], place(("qa", k)), ("qa", k), to_z(-(k - 3 * s)))
        for k in (2, -2, 1, -1):
            send(QB.at[at_z(-k)], place(("q", k)), ("q", k), to_z(-k))

    def q_far(s):
        total = Q[at_z(-3 * s)]
        for k in (4, 5, 6) if s > 0 else (-4, -5):
            need(("qa", k))
            total = total + unpack(place(("qa", k))[...])
        QS[0 if s > 0 else 1] = pack(total)
        send(QS.at[0 if s > 0 else 1], place(("q", 3 * s)), ("q", 3 * s), to_z(-3 * s))

    def q_sum():
        total = Q[z]
        for k in (1, -1, 2, -2, 3, -3):
            need(("q", k))
            total = total + unpack(place(("q", k))[...])
        state["old"] = total

    def turn(js):
        loaded("rows")
        reach = (1, -1, 2, -2, 3, -3) if 0 in js else (4, -4, 5, -5, 6, -6)
        for side in (0, 1):
            for k in reach:
                need(("r", k, side))
        need(("r", 0, 1))
        for j in js:
            pair = (z // 2 + j + 6) % 6
            block = R[pl.ds(2 * pair, 2)].reshape(128, 384)
            RT[:, pl.ds(pl.multiple_of(128 * pair, 128), 128)] = block.T

    def whiten(b):
        at, end = slice(256 * b, 256 * b + 256), 256 * b + 256
        WH[:, at] = dot(RT[:, :end], W[at, :end], ((1,), (1,))).astype(BF)

    def back(b):
        at = slice(256 * b, 256 * b + 256)
        hi, lo = split2(dot(WH[:, 256 * b :], Wm[256 * b :, at]))
        Y[:384, at] = hi
        Y[384:, at] = lo

    def gram(n):
        for side in (0, 1):
            for k in (0, 1, -1, 2, -2, 3, -3, 4):
                need(("s", k, side))
        at = slice(256 * n, 256 * n + 256)
        both = dot(Y[...], C[:, :, :, :, at].reshape(768, 256))
        new_o[:, at] = OLD[:, at] + (both[:384] + both[384:])

    def products():
        for k in (0, 1, -1, 2, -2, 3, -3, 4):
            need(("gs", k))
        total = state["old"]
        at = pl.multiple_of(col * 16, 16)
        for first in (0, 384):
            total = total + unpack(dot(Y[pl.ds(first + at, 16), :], GF[...].reshape(768, 128)))
        prod_o[...] = total

    tasks = dict(
        g=g_share, g1=g_x, g2=g_z, g3=g_y, gs=g_core, p1=q_x, psum=q_sum, mask=mask, prod=products,
        c4_0=lambda: last_cols(0), c4_1=lambda: last_cols(1), p2a=lambda: q_far(1), p2b=lambda: q_far(-1),
        turnA=lambda: turn((0, 1, -1)), turnB=lambda: turn((2, -2, 3)),
    )
    for step in ORDER:
        if step in tasks:
            tasks[step]()
        elif isinstance(step, str):
            what, i = step[:-1], int(step[-1])
            dict(sold=old_products, white=whiten, back=back, gram=gram)[what](i)
        else:
            came(step)
    for copy in sent:
        copy.wait_send()


def write_out(new_v, prod_v, new_h, prod_h, sems):
    copies = [pltpu.make_async_copy(prod_v, prod_h, sems.at[4])]
    for i in range(4):
        rows = pl.ds(96 * i, 96)
        copies.append(pltpu.make_async_copy(new_v.at[rows], new_h.at[rows], sems.at[i]))
    for copy in copies:
        copy.start()
    for copy in copies:
        copy.wait()


def body(design_rows, design_cols, whitening, epoch_mask, normal_old, probes):
    vmem = pl.BlockSpec(memory_space=pltpu.VMEM)
    hbm = pl.BlockSpec(memory_space=pltpu.HBM)
    new, products = pl.pallas_call(
        kernel,
        out_shape=(pltpu.VMEM((384, 1024), F32), pltpu.VMEM((16, 64), F32)),
        in_specs=[hbm] * 6,
        out_specs=(vmem, vmem),
        scratch_shapes=[
            pltpu.VMEM((NZ, 2, 32, 384), BF),
            pltpu.VMEM((384, 768), BF),
            pltpu.VMEM((2, NY, 2, 24, 1024), BF),
            pltpu.VMEM((768, 768), BF),
            pltpu.VMEM((768, 768), BF),
            pltpu.VMEM((384, 768), BF),
            pltpu.VMEM((768, 768), BF),
            pltpu.VMEM((384, 1024), F32),
            pltpu.VMEM((64, 1024), F32),
            pltpu.VMEM((NZ, 2, 16, 128), BF),
            pltpu.VMEM((NZ, 16, 128), BF),
            pltpu.VMEM((NZ, 16, 64), F32),
            pltpu.VMEM((NZ, 16, 128), BF),
            pltpu.VMEM((11, 16, 128), BF),
            pltpu.VMEM((2, 16, 128), BF),
            pltpu.VMEM((3, 24, 128), BF),
            pltpu.VMEM((3, 2, 24, 128), BF),
            pltpu.VMEM((5, 2, 24, 128), BF),
            pltpu.VMEM((2, NY, 2, 24, 128), BF),
            pltpu.VMEM((1, 128), jnp.int32),
            pltpu.SemaphoreType.DMA((128,)),
            pltpu.SemaphoreType.DMA((128,)),
            pltpu.SemaphoreType.DMA((6,)),
        ],
        compiler_params=pltpu.CompilerParams(
            collective_id=0, has_side_effects=True, vmem_limit_bytes=56 * 2**20
        ),
        name="normal_update",
    )(
        design_rows,
        design_cols,
        whitening,
        epoch_mask.reshape(1, 128),
        normal_old,
        probes.T,
    )
    return pl.pallas_call(
        write_out,
        out_shape=(
            jax.ShapeDtypeStruct((384, 1024), F32),
            jax.ShapeDtypeStruct((16, 64), F32),
        ),
        in_specs=[vmem, vmem],
        out_specs=(hbm, hbm),
        scratch_shapes=[pltpu.SemaphoreType.DMA((5,))],
        compiler_params=pltpu.CompilerParams(vmem_limit_bytes=4 * 2**20),
        name="write_out",
    )(new, products)


def solution(mesh):
    placed = (P("col", "row"), P("row", "col"), P(), P(), P("row", "col"), P("col", None))
    return jax.shard_map(
        body,
        mesh=mesh,
        in_specs=placed,
        out_specs=(P("row", "col"), P(("row", "col"), None)),
        check_vma=False,
    )
```

```python
import jax
import jax.numpy as jnp
from jax import lax
from jax.experimental import pallas as pl
from jax.experimental.pallas import tpu as pltpu
from jax.sharding import PartitionSpec as P

MESH = pl.DeviceIdType.MESH
COMP = 6
NZ, NY = 12, 8
BF, F32 = jnp.bfloat16, jnp.float32


def split2(x):
    hi = x.astype(BF)
    return hi, (x - hi.astype(F32)).astype(BF)


def dot(a, b, dims=((1,), (0,))):
    return lax.dot_general(a, b, (dims, ((), ())), preferred_element_type=F32)


def pack(x):
    return jnp.concatenate(split2(x), axis=-1)


def unpack(x):
    x = x.astype(F32)
    return x[..., :64] + x[..., 64:]


class Names(dict):
    def __missing__(self, key):
        self[key] = len(self)
        return self[key]


ROWS_ACROSS, ROWS_DIRECT = (3, -3), (2, -2, 1, -1)
COLS_ACROSS, COLS_DIRECT = (2, -2, 1, -1), ()
FIRST = (
    ("c", -1, 0), ("r", 3, 0), ("r", -3, 0), ("r", 1, 0), ("c", 1, 0), ("r", 2, 0),
    ("r", 0, 1), ("c", -2, 0), ("r", -2, 0), ("c", 2, 0), ("c", 0, 1), ("r", -1, 0),
)
EARLY = 10
ORDER = (
    "g", "mask", "sold0", ("c", -1, 0), ("r", 0, 1), ("c", 1, 0),
    "sold1", "sold2", "g1", ("c", -2, 0), ("c", 2, 0), ("r", 3, 0),
    ("r", -3, 0), "g2", ("c", 0, 1), ("c", 1, 1), ("c", -1, 1), "p1",
    ("c", -3, 0), "c4_0", ("c", 3, 0), ("c", -2, 1), ("r", 3, 1), ("c", 2, 1),
    ("r", -3, 1), "turnA", "p2b", "p2a", "g3", ("c", -3, 1),
    ("c", 3, 1), "c4_1", "turnB", "white0", "white1", "white2",
    "back2", "back1", "back0", "gs", "gram0", "gram1",
    "gram2", "gram3", "psum", "prod",
)


def kernel(
    rows_h, cols_h, w_h, mask_h, old_h, prob_h, new_o, left_o, old_o, g_o,
    R, RT, C, W, Wm, WH, Y, OLD, PR, PB, PX, Q, QB, QR, QS, GX, GS, GZ, GF, MASK, ss, rs, ls,
):
    row, col = lax.axis_index("row"), lax.axis_index("col")
    core, y, xh = row % 2, (row // 2) % NY, row // (2 * NY)
    z, xl = col // 2, col % 2

    def at_z(k):
        return (z + k + NZ) % NZ

    def at_y(k):
        return (y + k + NY) % NY

    def to_z(k):
        return (row, at_z(k) * 2 + xl)

    def to_y(k):
        return ((xh * NY + at_y(k)) * 2 + core, col)

    other_row = ((1 - xh) * NY + y) * 2 + core
    to_xl = (row, z * 2 + 1 - xl)
    to_xh = (other_row, col)
    to_diagonal = (other_row, z * 2 + 1 - xl)
    to_core = ((xh * NY + y) * 2 + 1 - core, col)

    barrier = pltpu.get_barrier_semaphore()
    others = [to_z(k) for k in (1, -1, 2, -2, 3, -3)] + [to_y(k) for k in (1, -1, 2, -2)]
    others += [to_xl, to_xh, to_diagonal, to_core]
    for other in others:
        pl.semaphore_signal(barrier, inc=1, device_id=other, device_id_type=MESH)

    loads = {
        name: pltpu.make_async_copy(src, dst, ls.at[i])
        for i, (name, src, dst) in enumerate(
            (
                ("cols", cols_h, C.at[xh, y, core]),
                ("probes", prob_h, PR),
                ("rows", rows_h, R.at[z, xl]),
                ("mask", mask_h, MASK),
                ("whitening", w_h, W),
                ("old", old_h, OLD),
            )
        )
    }
    for load in loads.values():
        load.start()

    sems, sent, seen, state = Names(), [], set(), {}

    def loaded(name):
        if name not in seen:
            seen.add(name)
            loads[name].wait()

    loaded("cols")
    loaded("probes")
    phi, plo = split2(PR[...])
    state["phi"], state["both"] = phi, jnp.concatenate([phi, plo], axis=0)
    state["mine"] = unpack(dot(C[xh, y, core], state["both"], ((1,), (1,))))
    GS[0, 0] = pack(state["mine"])

    def mask():
        loaded("mask")
        loaded("whitening")
        obs = lax.broadcasted_iota(jnp.int32, (768, 128), 0)
        first = COMP * lax.broadcasted_iota(jnp.int32, (768, 128), 1)
        keep = (obs >= first) & (obs < first + COMP)
        kept = jnp.sum(jnp.where(keep, MASK[...].astype(F32), 0.0), axis=1, keepdims=True)
        Wm[...] = W[...] * kept.astype(BF)

    pl.semaphore_wait(barrier, len(others))

    def send(src, dst, name, device):
        copy = pltpu.make_async_remote_copy(
            src_ref=src,
            dst_ref=dst,
            send_sem=ss.at[len(sent)],
            recv_sem=rs.at[sems[name]],
            device_id=device,
            device_id_type=MESH,
        )
        copy.start(priority=0)
        sent.append(copy)

    def place(name):
        kind, k, *side = name
        if kind == "r":
            at = (at_z(k), xl if side[0] == 0 else 1 - xl)
            return R.at[(*at, pl.ds(0 if k > 0 else 16, 16))] if abs(k) == 6 else R.at[at]
        if kind in ("c", "s"):
            at = (xh if side[0] == 0 else 1 - xh, at_y(k), core if kind == "c" else 1 - core)
            if kind == "c" and abs(k) == 4:
                return C.at[(*at, slice(None), pl.ds(0 if k > 0 else 512, 512))]
            return C.at[at]
        if kind == "gx":
            return GX.at[k]
        if kind in ("ga", "gb"):
            return GZ.at[{"ga": {-1: 0, 1: 1, 2: 2}, "gb": {4: 3, -4: 4}}[kind][k]]
        if kind == "gf":
            if abs(k) == 4:
                return GF.at[xh if k > 0 else 1 - xh, at_y(k), core]
            return GF.at[:, at_y(k), core]
        if kind == "gs":
            return GF.at[:, at_y(k), 1 - core]
        if kind == "px":
            return PX
        if kind == "qa":
            return QR.at[{4: 0, 5: 1, 6: 2, -4: 3, -5: 4}[k]]
        return QR.at[{1: 5, -1: 6, 2: 7, -2: 8, 3: 9, -3: 10}[k]]

    def need(name):
        if name not in seen:
            seen.add(name)
            ref = place(name)
            pltpu.make_async_remote_copy(
                src_ref=ref, dst_ref=ref, send_sem=ss.at[0], recv_sem=rs.at[sems[name]],
                device_id=to_core, device_id_type=MESH,
            ).wait_recv()

    def buf(kind, k, side):
        if kind == "r":
            return R.at[at_z(k), xl if side == 0 else 1 - xl]
        return C.at[xh if side == 0 else 1 - xh, at_y(k), core]

    def relay_rows(k, side):
        s = 1 if k > 0 else -1
        b = buf("r", k, side)
        half = b.at[pl.ds(0 if s > 0 else 16, 16)]
        send(half, half, ("r", 6 * s, side), to_z(-3 * s))
        send(b, b, ("r", 5 * s, side), to_z(-2 * s))
        send(b, b, ("r", 4 * s, side), to_z(-s))

    def relay_cols(k, side):
        s = 1 if k > 0 else -1
        b = buf("c", k, side)
        half = b.at[:, pl.ds(0 if s > 0 else 512, 512)]
        send(half, half, ("c", 4 * s, side), to_y(-2 * s))
        send(b, b, ("c", 3 * s, side), to_y(-s))

    def to_sibling(k, side):
        b = buf("c", k, side)
        send(b, b, ("s", k, side), to_core)

    def came(name):
        kind, k, side = name
        need(name)
        b = buf(kind, k, side)
        if kind == "r":
            if side == 0 and k in ROWS_ACROSS and abs(k) != 3:
                send(b, b, ("r", k, 1), to_xl)
            if abs(k) == 3:
                relay_rows(k, side)
                if side == 0 and k in ROWS_ACROSS:
                    send(b, b, ("r", k, 1), to_xl)
            if side == 1 and k == 0:
                for d in ROWS_DIRECT:
                    send(b, b, ("r", -d, 1), to_z(d))
        else:
            if side == 0 and k in COLS_ACROSS:
                send(b, b, ("c", k, 1), to_xh)
            if abs(k) == 2:
                relay_cols(k, side)
            if side == 1 and k == 0:
                for d in COLS_DIRECT:
                    send(b, b, ("c", -d, 1), to_y(d))
            to_sibling(k, side)

    def last_cols(side):
        need(("c", 4, side))
        need(("c", -4, side))
        to_sibling(4, side)

    def start(name):
        kind, k, side = name
        if kind == "c":
            device = to_xh if side else to_y(-k)
            send(cols_h, C.at[xh, y, core], name, device)
        else:
            device = to_xl if side else to_z(-k)
            send(rows_h, R.at[z, xl], name, device)

    for name in FIRST[:EARLY]:
        start(name)

    def g_share():
        for i, device in enumerate((to_xl, to_xh, to_diagonal)):
            send(GS.at[0, 0], GX.at[i], ("gx", i), device)
        for name in FIRST[EARLY:]:
            start(name)
        send(cols_h, C.at[xh, y, core], ("s", 0, 0), to_core)

    def g_x():
        for i in range(3):
            need(("gx", i))
        state["mine"] = state["mine"] + unpack(GX[0])
        state["theirs"] = unpack(GX[1]) + unpack(GX[2])
        GS[1, 0] = pack(state["mine"])
        GS[1, 1] = pack(state["theirs"])
        for k in (2, 1, -1):
            send(GS.at[1], place(("ga", k)), ("ga", k), to_z(-k))

    def g_add(names):
        for name in names:
            need(name)
            got = place(name)
            state["mine"] = state["mine"] + unpack(got[0])
            state["theirs"] = state["theirs"] + unpack(got[1])

    def g_z():
        g_add([("ga", k) for k in (1, -1, 2)])
        GS[2, 0] = pack(state["mine"])
        GS[2, 1] = pack(state["theirs"])
        for k in (4, -4):
            send(GS.at[2], place(("gb", k)), ("gb", k), to_z(-k))

    def g_y():
        g_add([("gb", k) for k in (4, -4)])
        GF[xh, y, core] = pack(state["mine"])
        GF[1 - xh, y, core] = pack(state["theirs"])
        for k in (1, -1, 2, -2):
            need(("c", k, 0))
        for k in (4, -4):
            b = GF.at[xh if k > 0 else 1 - xh, y, core]
            send(b, b, ("gf", k), to_y(-k))
        for k in (3, -3, 2, -2, 1, -1):
            send(GF.at[:, y, core], GF.at[:, y, core], ("gf", k), to_y(-k))

    def g_core():
        for k in (0, 1, -1, 2, -2, 3, -3, 4):
            if k:
                need(("gf", k))
            if k == 4:
                need(("gf", -4))
            b = GF.at[:, at_y(k), core]
            send(b, b, ("gs", k), to_core)

    def old_products(i):
        if i == 0:
            loaded("old")
        at = pl.ds(128 * i, 128)
        hi, lo = split2(OLD[at])
        PB[4 * i : 4 * i + 4] = pack(
            unpack(dot(hi, state["both"], ((1,), (1,)))) + dot(lo, state["phi"], ((1,), (1,)))
        ).reshape(4, 2, 16, 128)
        if i == 2:
            send(PB.at[:, 1 - xl], PX, ("px", 0), to_xl)

    def q_x():
        need(("px", 0))
        Q[...] = unpack(PB[:, xl]) + unpack(PX[...])
        QB[...] = pack(Q[...])
        for k in (6, 5, 4, -5, -4):
            s = 1 if k > 0 else -1
            send(QB.at[at_z(-k)], place(("qa", k)), ("qa", k), to_z(-(k - 3 * s)))
        for k in (2, -2, 1, -1):
            send(QB.at[at_z(-k)], place(("q", k)), ("q", k), to_z(-k))

    def q_far(s):
        total = Q[at_z(-3 * s)]
        for k in (4, 5, 6) if s > 0 else (-4, -5):
            need(("qa", k))
            total = total + unpack(place(("qa", k))[...])
        QS[0 if s > 0 else 1] = pack(total)
        send(QS.at[0 if s > 0 else 1], place(("q", 3 * s)), ("q", 3 * s), to_z(-3 * s))

    def q_sum():
        total = Q[z]
        for k in (1, -1, 2, -2, 3, -3):
            need(("q", k))
            total = total + unpack(place(("q", k))[...])
        state["old"] = total

    def turn(js):
        loaded("rows")
        reach = (1, -1, 2, -2, 3, -3) if 0 in js else (4, -4, 5, -5, 6, -6)
        for side in (0, 1):
            for k in reach:
                need(("r", k, side))
        need(("r", 0, 1))
        for j in js:
            pair = (z // 2 + j + 6) % 6
            block = R[pl.ds(2 * pair, 2)].reshape(128, 384)
            RT[:, pl.ds(pl.multiple_of(128 * pair, 128), 128)] = block.T

    def whiten(b):
        at, end = slice(256 * b, 256 * b + 256), 256 * b + 256
        WH[:, at] = dot(RT[:, :end], W[at, :end], ((1,), (1,))).astype(BF)

    def back(b):
        at = slice(256 * b, 256 * b + 256)
        hi, lo = split2(dot(WH[:, 256 * b :], Wm[256 * b :, at]))
        Y[:384, at] = hi
        Y[384:, at] = lo

    def gram(n):
        for side in (0, 1):
            for k in (0, 1, -1, 2, -2, 3, -3, 4):
                need(("s", k, side))
        at = slice(256 * n, 256 * n + 256)
        both = dot(Y[...], C[:, :, :, :, at].reshape(768, 256))
        new_o[:, at] = OLD[:, at] + (both[:384] + both[384:])

    def products():
        at = pl.multiple_of(col * 16, 16)
        left_o[:16] = Y[pl.ds(at, 16), :]
        left_o[16:] = Y[pl.ds(384 + at, 16), :]
        old_o[...] = state["old"]
        for k in (0, 1, -1, 2, -2, 3, -3, 4):
            need(("gs", k))
        g_o[...] = GF[...].reshape(768, 128)

    tasks = dict(
        g=g_share, g1=g_x, g2=g_z, g3=g_y, gs=g_core, p1=q_x, psum=q_sum, mask=mask, prod=products,
        c4_0=lambda: last_cols(0), c4_1=lambda: last_cols(1), p2a=lambda: q_far(1), p2b=lambda: q_far(-1),
        turnA=lambda: turn((0, 1, -1)), turnB=lambda: turn((2, -2, 3)),
    )
    for step in ORDER:
        if step in tasks:
            tasks[step]()
        elif isinstance(step, str):
            what, i = step[:-1], int(step[-1])
            dict(sold=old_products, white=whiten, back=back, gram=gram)[what](i)
        else:
            came(step)
    for copy in sent:
        copy.wait_send()


def write_out(new_v, left_v, old_v, g_v, new_h, prod_h, prod_v, sems):
    copies = []
    for i in range(4):
        rows = pl.ds(96 * i, 96)
        copies.append(pltpu.make_async_copy(new_v.at[rows], new_h.at[rows], sems.at[i]))
    for copy in copies:
        copy.start()
    both = unpack(dot(left_v[...], g_v[...]))
    prod_v[...] = old_v[...] + both[:16] + both[16:]
    copies.append(pltpu.make_async_copy(prod_v, prod_h, sems.at[4]))
    copies[4].start()
    for copy in copies:
        copy.wait()


def body(design_rows, design_cols, whitening, epoch_mask, normal_old, probes):
    vmem = pl.BlockSpec(memory_space=pltpu.VMEM)
    hbm = pl.BlockSpec(memory_space=pltpu.HBM)
    parts = pl.pallas_call(
        kernel,
        out_shape=(
            pltpu.VMEM((384, 1024), F32),
            pltpu.VMEM((32, 768), BF),
            pltpu.VMEM((16, 64), F32),
            pltpu.VMEM((768, 128), BF),
        ),
        in_specs=[hbm] * 6,
        out_specs=(vmem,) * 4,
        scratch_shapes=[
            pltpu.VMEM((NZ, 2, 32, 384), BF),
            pltpu.VMEM((384, 768), BF),
            pltpu.VMEM((2, NY, 2, 24, 1024), BF),
            pltpu.VMEM((768, 768), BF),
            pltpu.VMEM((768, 768), BF),
            pltpu.VMEM((384, 768), BF),
            pltpu.VMEM((768, 768), BF),
            pltpu.VMEM((384, 1024), F32),
            pltpu.VMEM((64, 1024), F32),
            pltpu.VMEM((NZ, 2, 16, 128), BF),
            pltpu.VMEM((NZ, 16, 128), BF),
            pltpu.VMEM((NZ, 16, 64), F32),
            pltpu.VMEM((NZ, 16, 128), BF),
            pltpu.VMEM((11, 16, 128), BF),
            pltpu.VMEM((2, 16, 128), BF),
            pltpu.VMEM((3, 24, 128), BF),
            pltpu.VMEM((3, 2, 24, 128), BF),
            pltpu.VMEM((5, 2, 24, 128), BF),
            pltpu.VMEM((2, NY, 2, 24, 128), BF),
            pltpu.VMEM((1, 128), jnp.int32),
            pltpu.SemaphoreType.DMA((128,)),
            pltpu.SemaphoreType.DMA((128,)),
            pltpu.SemaphoreType.DMA((6,)),
        ],
        compiler_params=pltpu.CompilerParams(
            collective_id=0, has_side_effects=True, vmem_limit_bytes=56 * 2**20
        ),
        name="normal_update",
    )(
        design_rows,
        design_cols,
        whitening,
        epoch_mask.reshape(1, 128),
        normal_old,
        probes.T,
    )
    return pl.pallas_call(
        write_out,
        out_shape=(
            jax.ShapeDtypeStruct((384, 1024), F32),
            jax.ShapeDtypeStruct((16, 64), F32),
        ),
        in_specs=[vmem] * 4,
        out_specs=(hbm, hbm),
        scratch_shapes=[pltpu.VMEM((16, 64), F32), pltpu.SemaphoreType.DMA((5,))],
        compiler_params=pltpu.CompilerParams(vmem_limit_bytes=4 * 2**20),
        name="write_out",
    )(*parts)


def solution(mesh):
    placed = (P("col", "row"), P("row", "col"), P(), P(), P("row", "col"), P("col", None))
    return jax.shard_map(
        body,
        mesh=mesh,
        in_specs=placed,
        out_specs=(P("row", "col"), P(("row", "col"), None)),
        check_vma=False,
    )
```
